32 devices in a mesh: prow: 2 (over x), pcol: 16 (over z, y, core).
Axes of the slice: x: 2, y: 2, z: 4, core: 2. Of those that a mesh axis runs over, the one named last changes fastest.
Arguments:
- segment: float32 [8, 2, 512, 8192], P(None, 'prow', None, 'pcol'), as said below
- above_rows: float32 [2048, 8192], P('prow', 'pcol'), may hold values from -6 to 6
- basis_rows: float32 [2048, 8192], P('prow', 'pcol'), may hold values from -6 to 6
- factors: float32 [2, 16, 512, 512], P(None, 'pcol'), as said below
- swap_counts: int32 [2, 16], replicated, may hold values from 0 to 256, as said below
Outputs:
- segment_out: float32 [8, 2, 512, 8192], P(None, 'prow', None, 'pcol')
- above_out: float32 [2048, 8192], P('prow', 'pcol')
- basis_out: float32 [2048, 8192], P('prow', 'pcol')
The draws below stay inside these ranges and needn't reach their ends.
Inputs may be any that keep to these rules, and one draw needn't show every extreme that they name: segment is upper quasi-triangular: below the diagonal it is nonzero only just under the diagonal, at odd rows, never in two rows in a row. Each factors[phase, k] is an orthogonal 512 x 512 matrix. `swap_counts`: a window is applied where its count is positive and left out where it is 0; the second phase's window 16 - 1 always has count 0.
All inputs are finite; a program needn't handle non-finite values.
Results may differ from the reference program's by a relative error of at most 0.000088.
Values sent between devices are 32-bit elements; how exact they have to be, the bound alone decides.
No kernel may reach another device: no remote copies, remote signals or barrier semaphores. Data moves between devices by JAX's collectives and lax.ppermute only.
A program may use at most 128 MiB of HBM per device.

```python
import jax
import jax.numpy as jnp
from jax import lax

W = 512
ABOVE = 2048
QROWS = 2048
SEG = 8192
N_PROW = 2
N_PCOL = 16


def draw_segment(key, part):
    layout = (N_PCOL // N_PROW, N_PROW, W, SEG)
    values = jax.random.normal(jax.random.fold_in(key, 1), layout, jnp.float32)
    row_index = (lax.broadcasted_iota(jnp.int32, layout, 0) * N_PROW + lax.broadcasted_iota(jnp.int32, layout, 1)) * W + lax.broadcasted_iota(jnp.int32, layout, 2)
    col_index = lax.broadcasted_iota(jnp.int32, layout, 3)
    subdiag = jax.random.randint(jax.random.fold_in(key, 2), layout, 0, 2)
    retain = (col_index >= row_index) | (col_index == row_index - 1) & (row_index % 2 == 1) & (subdiag == 1)
    return jnp.where(retain, values, 0.0).astype(jnp.float32)


def draw_factors(key, part):
    layout = (2, N_PCOL, W, W)
    raw_matrix = jax.random.normal(jax.random.fold_in(key, 1), layout, jnp.float32)
    orthogonal, upper_factor = jnp.linalg.qr(raw_matrix)
    diagonal_part = jnp.diagonal(upper_factor, axis1=-2, axis2=-1)
    column_signs = jnp.where(diagonal_part >= 0.0, 1.0, -1.0).astype(jnp.float32)
    return (orthogonal * column_signs[..., None, :]).astype(jnp.float32)


def draw_swap_counts(key, part):
    amount = jax.random.randint(jax.random.fold_in(key, 1), (2, N_PCOL), 1, W // 2 + 1)
    status = jax.random.randint(jax.random.fold_in(key, 2), (2, N_PCOL), 0, 4)
    counts_drawn = jnp.where(status < 3, amount, 0)
    phase_index = lax.broadcasted_iota(jnp.int32, (2, N_PCOL), 0)
    window_index = lax.broadcasted_iota(jnp.int32, (2, N_PCOL), 1)
    fullest = jax.random.randint(jax.random.fold_in(key, 3), (), 0, N_PCOL)
    counts_drawn = jnp.where((phase_index == 0) & (window_index == fullest), W // 2, counts_drawn)
    final_window = (phase_index == 1) & (window_index == N_PCOL - 1)
    return jnp.where(final_window, 0, counts_drawn).astype(jnp.int32)


def block_levels(rng, shape, pieces, least, largest):
    factor_of = 1.0
    for axis_at, blocks in pieces:
        draws = jax.random.uniform(jax.random.fold_in(jax.random.fold_in(rng, 6), axis_at), (blocks,), jnp.float32, least / len(pieces), largest / len(pieces))
        factor_of = factor_of * jnp.repeat(jnp.exp(draws), shape[axis_at] // blocks).reshape((-1,) + (1,) * (len(shape) - 1 - axis_at))
    return factor_of


def scatter_about(own_key, extent, scale, reach, split=(), kind=jnp.bfloat16):
    loudness = block_levels(own_key, extent, split, -0.22, 0.18) if split else 1.0
    entries = jax.random.normal(own_key, extent, jnp.float32) * scale * loudness
    return jnp.minimum(jnp.maximum(entries, -reach), reach).astype(kind)


def setup_inputs(seed: int = 0) -> dict:
    splits = jax.random.split(jax.random.key(seed), 6)
    segment = draw_segment(jax.random.fold_in(splits[5], 71), 0)
    above_rows = scatter_about(splits[1], (ABOVE, SEG), 1.0, 6.0, ((0, 2), (1, 16)), jnp.float32)
    basis_rows = scatter_about(splits[2], (QROWS, SEG), 1.0, 6.0, ((0, 2), (1, 16)), jnp.float32)
    factors = draw_factors(jax.random.fold_in(splits[5], 71), 0)
    swap_counts = draw_swap_counts(jax.random.fold_in(splits[5], 71), 0)
    return {"segment": segment, "above_rows": above_rows, "basis_rows": basis_rows, "factors": factors, "swap_counts": swap_counts}


HIGHEST = lax.Precision.HIGHEST

def active_factors(factor_stack, counts_row):
    window = factor_stack.shape[-1]
    identity = jnp.eye(window, dtype=factor_stack.dtype)
    return jnp.where((counts_row > 0)[:, None, None], factor_stack, identity)

def right_blocks(matrix, factor_stack):
    row_total = matrix.shape[0]
    block_count = factor_stack.shape[0]
    window = factor_stack.shape[1]
    grouped = matrix.reshape(row_total, block_count, window)
    result = jnp.einsum('rkw,kwv->rkv', grouped, factor_stack, precision=HIGHEST)
    return result.reshape(row_total, block_count * window)

def left_blocks(matrix, factor_stack):
    col_total = matrix.shape[1]
    block_count = factor_stack.shape[0]
    window = factor_stack.shape[1]
    grouped = matrix.reshape(block_count, window, col_total)
    result = jnp.einsum('kwv,kwc->kvc', factor_stack, grouped, precision=HIGHEST)
    return result.reshape(block_count * window, col_total)

def right_shifted(matrix, factor_stack):
    half_width = factor_stack.shape[1] // 2
    interior = right_blocks(matrix[:, half_width:-half_width], factor_stack)
    return jnp.concatenate([matrix[:, :half_width], interior, matrix[:, -half_width:]], axis=1)

def left_shifted(matrix, factor_stack):
    half_width = factor_stack.shape[1] // 2
    interior = left_blocks(matrix[half_width:-half_width], factor_stack)
    return jnp.concatenate([matrix[:half_width], interior, matrix[-half_width:]], axis=0)

def reference(segment, above_rows, basis_rows, factors, swap_counts):
    layout = segment.shape
    matrix_order = layout[0] * layout[1] * layout[2]
    square = segment.reshape(matrix_order, matrix_order)
    first_stack = active_factors(factors[0], swap_counts[0])
    second_stack = active_factors(factors[1][:-1], swap_counts[1][:-1])
    square = left_blocks(right_blocks(square, first_stack), first_stack)
    square = left_shifted(right_shifted(square, second_stack), second_stack)
    above_out = right_shifted(right_blocks(above_rows, first_stack), second_stack)
    basis_out = right_shifted(right_blocks(basis_rows, first_stack), second_stack)
    return (square.reshape(layout), above_out, basis_out)
```

```python
import functools

import jax
import jax.numpy as jnp
from jax import lax
from jax.experimental import pallas as pl
from jax.experimental.pallas import tpu as pltpu
from jax.sharding import PartitionSpec as P

GRID = ("prow", "pcol")
VMEM_LIMIT = 60 * 1024 * 1024


def split(value):
    high = value.astype(jnp.bfloat16)
    return high, (value - high.astype(jnp.float32)).astype(jnp.bfloat16)


def dot3(left, right):
    (lh, ll), (rh, rl) = left, right
    dot = functools.partial(jnp.dot, preferred_element_type=jnp.float32)
    return dot(lh, rh) + (dot(lh, rl) + dot(ll, rh))


PLANE, COL, PLANE0, NEWEST, MEMBER, SWAP_B, FIRST_IN, LAST_IN, LAST_LEVEL, USE_LAST, OWNS, COUNTS = range(12)


def call(kernel, info, grid, in_specs, out_specs, out_shape, scratch, args, alias=None, after=(), opens=False):
    count = len(args)
    after = [a for a in after if all(a is not arg for arg in args)]

    def run(*refs):
        kernel(*refs[: count + 1], *refs[count + 1 + len(after) :])

    return pl.pallas_call(
        run,
        grid_spec=pltpu.PrefetchScalarGridSpec(
            num_scalar_prefetch=1,
            grid=grid,
            in_specs=in_specs + [pl.BlockSpec(memory_space=pl.ANY)] * len(after),
            out_specs=out_specs,
            scratch_shapes=scratch,
        ),
        out_shape=out_shape,
        input_output_aliases=alias or {},
        compiler_params=pltpu.CompilerParams(vmem_limit_bytes=VMEM_LIMIT),
        cost_estimate=pl.CostEstimate(flops=10**14 if opens else 1, bytes_accessed=1, transcendentals=0),
    )(info, *args, *after)


def factor_kernel(paired, cols, info, factors, came, first, first_t, half_a, chain_b, prev, cur):
    window = first.shape[0]
    half = window // 2
    at = info[COL]
    rows = lax.broadcasted_iota(jnp.int32, (window, window), 0)
    lanes = lax.broadcasted_iota(jnp.int32, (window, window), 1)
    identity = (rows == lanes).astype(jnp.float32)
    own = jnp.where(info[COUNTS + at] > 0, factors[0, 0], identity)
    first[...] = own
    if paired:
        owner = at - lax.rem(at, 2) + info[PLANE]
        there = jnp.where(info[COUNTS + owner] > 0, came[...], identity)
        own = jnp.where(info[OWNS] == 1, own, there)
    own = own.T
    first_t[0] = own[:half]
    first_t[1] = own[half:]
    half_a[...] = jnp.where(info[MEMBER] == 1, own[half:], own[:half])
    on = (info[COUNTS + cols + at] > 0) & (at < cols - 1)
    own = jnp.where(on, factors[1, 0], identity)
    prev[...] = own[:, half:]
    cur[...] = own[:, :half]
    chain_b[...] = jnp.where(info[OWNS] == 1, own[:, :half], own[:, half:]).T


def gather_kernel(info, *refs):
    for place, piece in enumerate(refs[:-1]):
        refs[-1][place] = piece[...]


def first_kernel(joint, info, seg, col, factor, prev_top, *rest):
    sends, (last_top, col_h, col_l, carry) = rest[: 2 - joint], rest[2 - joint :]
    half = prev_top.shape[0]
    i = pl.program_id(0)

    @pl.when(i == 0)
    def _():
        col_h[...], col_l[...] = split(col[...])
        carry[...] = prev_top[...]

    mid = split(dot3(split(seg[...]), (col_h[...], col_l[...])))
    out = dot3(split(jnp.concatenate([factor[0], factor[1]], axis=0)), mid)
    sent = jnp.where(info[PLANE0] == 1, carry[...], out[:half])
    if joint:
        sends[0][0] = out[half:]
        sends[0][1] = sent
    else:
        sends[0][...] = out[half:]
        sends[1][...] = sent
    carry[...] = out[:half]
    last_top[...] = out[:half]


def second_kernel(begin, count, tail, info, factor, bottom, sent, got_bottom, got_top, *rest):
    left, right = rest[-2:]
    half = bottom.shape[0]

    @pl.when(pl.program_id(0) < count)
    def _():
        lower, upper = split(factor[info[SWAP_B]]), split(factor[1 - info[SWAP_B]])

        def stacked(one, other):
            return split(jnp.concatenate([one, other], axis=0))

        new_bottom = dot3(lower, stacked(bottom[...], got_top[...]))
        new_top = dot3(upper, stacked(got_bottom[...], sent[...]))
        passing = (info[PLANE0] == 1) & (begin + pl.program_id(0) == info[NEWEST] + 1)
        new_top = jnp.where(passing, sent[...], new_top)
        left[0] = new_bottom[:, :half]
        left[1] = new_top[:, :half]
        right[0] = new_bottom[:, half:]
        right[1] = new_top[:, half:]

    if tail:

        @pl.when(pl.program_id(0) == count)
        def _():
            left[0] = left[1] = rest[0][:, :half]
            right[0] = right[1] = rest[0][:, half:]


def split_columns(prev, cur, scratch):
    prev_h, prev_l, cur_h, cur_l = scratch
    prev_h[...], prev_l[...] = split(prev[...])
    cur_h[...], cur_l[...] = split(cur[...])


def columns(left_in, mine_left, mine_right, right_in, scratch, out):
    prev_h, prev_l, cur_h, cur_l = scratch
    half = mine_left.shape[1]

    def wide(one, other):
        return split(jnp.concatenate([one, other], axis=1))

    out[:, :half] = dot3(wide(left_in, mine_left), (prev_h[...], prev_l[...]))
    out[:, half:] = dot3(wide(mine_right, right_in), (cur_h[...], cur_l[...]))


def third_kernel(begin, last_unit, info, left, right, up_far, up_near, down_near, down_far, down_last, prev, cur, held, out, *scratch):
    del held
    e, h = pl.program_id(0), pl.program_id(1)

    @pl.when((e == 0) & (h == 0))
    def _():
        split_columns(prev, cur, scratch)

    left_in = jnp.where(info[FIRST_IN] == 1, up_far[...], up_near[...])
    far = jnp.where((info[USE_LAST] == 1) & (begin + e == last_unit) & (h == 1), down_last[...], down_far[...])
    right_in = jnp.where(info[LAST_IN] == 1, far, down_near[...])
    columns(left_in, left[...], right[...], right_in, scratch, out)


def last_kernel(info, top, up_far, up_near, down_near, prev, cur, held, out, *scratch):
    del held
    half = top.shape[0]
    split_columns(prev, cur, scratch)
    left_in = jnp.where(info[FIRST_IN] == 1, up_far[...], up_near[...])
    columns(left_in, top[:, :half], top[:, half:], down_near[...], scratch, out)

def rows_kernel(above_blocks, info, above, basis, col, left, right, col_h, col_l):
    half = left.shape[1]
    i = pl.program_id(0)

    @pl.when(i == 0)
    def _():
        col_h[...], col_l[...] = split(col[...])

    rows = jnp.where(i < above_blocks, above[...], basis[...])
    out = dot3(split(rows), (col_h[...], col_l[...]))
    left[...] = out[:, :half]
    right[...] = out[:, half:]


def rows_end_kernel(info, left, right, left_in, right_in, prev, cur, out, *scratch):
    @pl.when(pl.program_id(0) == 0)
    def _():
        split_columns(prev, cur, scratch)

    columns(left_in[...], left[...], right[...], right_in[...], scratch, out)


def whole(shape):
    return pl.BlockSpec(shape, lambda *_: (0,) * len(shape))


def body(segment, above_rows, basis_rows, factors, swap_counts):
    slots = segment.shape[0]
    window = segment.shape[2]
    half = window // 2
    planes = lax.axis_size("prow")
    cols = lax.axis_size("pcol")
    plane = lax.axis_index("prow")
    col = lax.axis_index("pcol")
    f32, bf = jnp.float32, jnp.bfloat16
    paired = planes == 2
    fold = next(size for size in (4, 2, 1) if slots % size == 0) if paired else 1
    group = planes * fold
    levels = slots // fold
    level = col // group
    newest = fold * level + fold - 1
    owner = plane if paired else (plane + planes - 1) % planes
    member = col % planes
    place = [
        plane,
        col,
        plane == 0,
        newest,
        member,
        (plane == 1) & paired,
        col % group == 0,
        col % group == group - 1,
        level == levels - 1,
        (plane == 0) & (level == levels - 2),
        member == plane,
    ]
    info = jnp.concatenate([jnp.stack([jnp.asarray(v, jnp.int32) for v in place]), swap_counts.reshape(-1)])

    def send(value, route):
        return lax.ppermute(value, GRID, [(a * cols + b, c * cols + d) for (a, b), (c, d) in route])

    everyone = [(p, c) for p in range(planes) for c in range(cols)]

    def along(value, step, wanted=lambda c: True):
        route = [((p, c), (p, c + step)) for p, c in everyone if 0 <= c + step < cols and wanted(c)]
        return send(value, route)

    def shape(*dims):
        return jax.ShapeDtypeStruct(dims, f32)

    last = []

    if paired:
        raw = factors[0, 0]
        came = send(raw, [((p, c), (p, c + 1 - 2 * p)) for p, c in everyone if c % 2 == p])
    else:
        came = factors[0, 0]
    own_first, full_first, half_a, chain_b, prev_own, cur = call(
        functools.partial(factor_kernel, paired, cols),
        info,
        (1,),
        [whole((2, 1, window, window)), whole((window, window))],
        [whole((window, window)), whole((2, half, window))]
        + [whole((half, window))] * 2
        + [whole((window, half))] * 2,
        [shape(window, window), shape(2, half, window)] + [shape(half, window)] * 2 + [shape(window, half)] * 2,
        [],
        (factors, came),
    )
    last.append(own_first)
    rows = lax.broadcasted_iota(jnp.int32, (window, half), 0)
    lanes = lax.broadcasted_iota(jnp.int32, (window, half), 1)

    def hopped(value, hop):
        return along(value, group, lambda c: c // group >= hop - 1)

    def chained(value):
        values = [value]
        for hop in range(1, levels):
            values.append(hopped(values[-1], hop))
        return values

    teams = [list(range(g * group, (g + 1) * group)) for g in range(cols // group)]
    if paired:
        pieces_b = chained(chain_b)
        first_factors = [lax.all_gather(v, "pcol", axis_index_groups=teams) for v in chained(half_a)]
    else:

        def shared(value, holder):
            value = jnp.where(member == holder, value, jnp.zeros_like(value))
            return lax.psum(value, "pcol", axis_index_groups=teams)

        full_first = shared(full_first, plane)
        first_factors = chained(full_first)
        both = jnp.stack([shared(chain_b, plane), shared(chain_b, owner)])
        second_factors = jnp.stack(chained(both), axis=1)

    def gather_second():
        out = call(
            gather_kernel,
            info,
            (1,),
            [whole((half, window))] * levels,
            whole((levels, half, window)),
            shape(levels, half, window),
            [],
            pieces_b,
            after=last[-1:],
        )
        last.append(out)
        return lax.all_gather(out, "pcol", axis_index_groups=teams)

    came_prev = along(prev_own, 1)
    prev = jnp.where(col == 0, (rows == lanes + half).astype(f32), came_prev)

    seg = segment.reshape(slots * window, window)

    def slot_of(t, f):
        return lax.rem(f[NEWEST] - t + slots, slots)

    def first_step(batch, prev_top, joint, after, opens):
        count, begin = len(batch), batch[0]
        factor = full_first if begin == 0 else first_factors[begin // fold]
        place = 0 if begin == 0 else fold - 1 - begin % fold
        if joint:
            specs = [pl.BlockSpec((None, 2, half, window), lambda i, f: (i, 0, 0, 0))]
            shapes = [shape(count, 2, half, window)]
        else:
            specs = [pl.BlockSpec((None, None, half, window), lambda i, f: (i, 0, 0, 0))] * 2
            shapes = [shape(count, 1, half, window)] * 2
        outs = call(
            functools.partial(first_kernel, joint),
            info,
            (count,),
            [
                pl.BlockSpec((window, window), lambda i, f: (slot_of(begin + i, f), 0)),
                whole((window, window)),
                pl.BlockSpec((2, half, window), lambda i, f: (place - i, 0, 0)),
                whole((half, window)),
            ],
            specs + [whole((half, window))],
            shapes + [shape(half, window)],
            [pltpu.VMEM((window, window), bf)] * 2 + [pltpu.VMEM((half, window), f32)],
            (seg, own_first, factor, prev_top),
            after=[*last[-1:], *after],
            opens=opens,
        )
        return outs[:-1], outs[-1]

    def exchange(batch, sends):
        down, up = [], []
        for p, c in everyone:
            places = [fold * (c // group) + fold - 1 - t for t in batch]
            tiles = [at * planes + p for at in places if at >= 0]
            if any(tile <= c and tile < cols - 1 for tile in tiles):
                down.append(((p, c), ((p + 1) % planes, c)))
            if any((tile if p else tile + planes) <= c for tile in tiles):
                up.append(((p, c), ((p - 1) % planes, c)))
        if len(sends) == 1:
            return [send(sends[0], sorted(set(down + up)))]
        return [send(sends[0], down), send(sends[1], up)]

    def second_step(batch, size, at, sends, gots, held, ended, after, opens):
        count, begin = len(batch), batch[0]
        hop, place = begin // fold, fold - 1 - begin % fold
        inner = lambda i: jnp.minimum(i, count - 1)
        piece = lambda k: pl.BlockSpec((None, None, half, window), lambda i, f: (inner(i), k, 0, 0))
        pieces = [piece(0), piece(len(sends) % 2)]
        ends = [pl.BlockSpec((2, half, half), lambda i, f: (at + i, 0, 0))] * 2
        extra = [whole((half, window))] if ended else [pl.BlockSpec(memory_space=pl.ANY)] * len(held)
        return call(
            functools.partial(second_kernel, begin, count, bool(ended)),
            info,
            (count + len(ended),),
            [pl.BlockSpec((2, None, half, window), lambda i, f: (place - inner(i), hop, 0, 0))] + pieces + pieces + extra,
            ends,
            [shape(2 * size, half, half)] * 2,
            [],
            (second_factors, sends[0], sends[-1], gots[0], gots[-1], *ended, *held),
            {6 + k: k for k in range(len(held))},
            [*last[-1:], *after],
            opens,
        )

    split_scratch = [pltpu.VMEM((window, half), bf)] * 4

    counts = (above_rows.shape[0], basis_rows.shape[0])
    deep = window if all(n % window == 0 for n in counts) else half
    above_blocks, basis_blocks = (n // deep for n in counts)

    def rows_step(after=(), opens=False):
        tall = pl.BlockSpec((deep, half), lambda i, f: (i, 0))
        blocks = above_blocks + basis_blocks
        return call(
            functools.partial(rows_kernel, above_blocks),
            info,
            (blocks,),
            [
                pl.BlockSpec((deep, window), lambda i, f: (jnp.minimum(i, above_blocks - 1), 0)),
                pl.BlockSpec((deep, window), lambda i, f: (jnp.maximum(i - above_blocks, 0), 0)),
                whole((window, window)),
            ],
            [tall] * 2,
            [shape(blocks * deep, half)] * 2,
            [pltpu.VMEM((window, window), bf)] * 2,
            (above_rows, basis_rows, own_first),
            after=[*last[-1:], *after],
            opens=opens,
        )

    def rows_end(first, blocks, parts):
        tall = pl.BlockSpec((deep, half), lambda i, f: (first + i, 0))
        return call(
            rows_end_kernel,
            info,
            (blocks,),
            [tall] * 4 + [whole((window, half))] * 2,
            pl.BlockSpec((deep, window), lambda i, f: (i, 0)),
            shape(blocks * deep, window),
            split_scratch,
            (*parts, prev, cur),
            after=last[-1:],
        )

    lefts, rights, ups, downs = ([None] * slots for _ in range(4))

    def third_step(batch, held, after, opens):
        begin = batch[0]
        fresh = held is None
        parts = [lefts[begin], rights[begin]]
        parts.append(ups[begin - fold] if begin >= fold else (no_strips, 0))
        parts += [ups[begin], downs[begin], downs[(begin + fold) % slots]]
        piece = lambda at: pl.BlockSpec((None, half, half), lambda e, h, f: (2 * (at + e) + h, 0, 0))

        def out_block(e, h, f):
            slot = slot_of(begin + e, f)
            upper = lax.rem(slot + f[PLANE0], slots)
            return (jnp.where(h == 0, 2 * slot + 1, 2 * upper), 0)

        args = [array for array, _ in parts]
        ending = slots - fold in batch
        tail_row = 2 * ending_strips[2] if ending else 0
        return call(
            functools.partial(third_kernel, begin, slots - fold),
            info,
            (len(batch), 2),
            [piece(at) for _, at in parts]
            + [pl.BlockSpec((None, half, half), lambda e, h, f: (tail_row, 0, 0))]
            + [whole((window, half))] * 2
            + [pl.BlockSpec(memory_space=pl.ANY)],
            pl.BlockSpec((half, window), out_block),
            shape(*seg.shape),
            split_scratch,
            (*args, ending_strips[1] if ending else args[0], prev, cur, args[0] if fresh else held),
            None if fresh else {10: 0},
            [*last[-1:], *after],
            opens,
        )

    def last_step(held):
        quarter = lambda at: pl.BlockSpec((None, half, half), lambda i, f: (at, 0, 0))
        array, at = ups[slots - fold]

        def out_block(i, f):
            return (jnp.where((f[LAST_LEVEL] == 1) & (f[PLANE0] == 1), 0, 2 * slot_of(slots - 1, f) + 1), 0)

        return call(
            last_kernel,
            info,
            (1,),
            [whole((half, window)), quarter(2 * at + 1)] + [quarter(2 * ending_strips[2])] * 2
            + [whole((window, half))] * 2
            + [pl.BlockSpec(memory_space=pl.ANY)],
            pl.BlockSpec((half, window), out_block),
            shape(*seg.shape),
            split_scratch,
            (tops[-1], array, *ending_strips[:2], prev, cur, held),
            {7: 0},
            last[-1:],
        )

    tops, sent, got, made = [jnp.zeros((half, window), f32)], {}, {}, {}
    no_strips = jnp.zeros((2 * slots, half, half), f32)

    def do_first(batch, after=(), opens=False):
        sent[batch[0]], top = first_step(batch, tops[-1], paired and batch[0] > 0, after, opens)
        tops.append(top)
        last.append(top)
        got[batch[0]] = exchange(batch, sent[batch[0]])

    def do_second(batch, strip, ended=(), after=(), opens=False):
        begin = batch[0]
        held = made.get(strip[0], ())
        made[strip[0]] = second_step(
            batch, len(strip) + len(ended), begin - strip[0], sent[begin], got[begin], held, ended, after, opens
        )
        last.append(made[strip[0]][0])
        if batch[-1] == strip[-1]:
            left, right = made[strip[0]]
            up, down = along(right, 1), along(left, -1)
            for place, t in enumerate(strip):
                lefts[t], rights[t] = (left, place), (right, place)
                ups[t], downs[t] = (up, place), (down, place)
            return up, down, len(strip)

    out = [None]

    def do_third(batch, after=(), opens=False):
        out[0] = third_step(batch, out[0], after, opens)
        last.append(out[0])

    def do_last():
        out[0] = last_step(out[0])
        last.append(out[0])

    def do_rows():
        left, right = rows_step(opens=True)
        last.append(left)
        return left, right, along(right, 1), along(left, -1)

    def do_rows_end():
        for first, blocks in ((0, above_blocks), (above_blocks, basis_blocks)):
            row_ends.append(rows_end(first, blocks, parts))
            last.append(row_ends[-1])

    row_ends = []
    if paired and fold == 4 and levels == 2:
        do_first([0])
        parts = do_rows()
        do_first([1], [came_prev, *got[0]])
        do_first([2, 3], opens=True)
        do_first([4, 5], got[1], opens=True)
        second_factors = gather_second()
        do_first([6, 7], [*got[2], *parts[2:]], opens=True)
        for batch in ([0], [1], [2, 3]):
            do_second(batch, [0, 1, 2, 3])
        ending_strips = do_second([4, 5], [4, 5], ended=[tops[-1]], opens=True)
        do_rows_end()
        do_second([6, 7], [6, 7], after=[*ups[0][:1], *downs[0][:1]])
        do_third([0, 1], opens=True)
        do_third([4, 5])
        do_last()
        do_third([2, 3])
        do_third([6, 7])
    else:
        parts = do_rows()
        for t in range(slots):
            do_first([t])
        if paired:
            second_factors = gather_second()
        for t in range(slots):
            ending_strips = do_second([t], [t], ended=[tops[-1]] if t == slots - 1 else ())
        for t in range(slots - 1):
            do_third([t])
        do_last()
        do_third([slots - 1])
        do_rows_end()
    return (out[0].reshape(segment.shape), *row_ends)


def solution(mesh):
    placed = (
        P(None, "prow", None, "pcol"),
        P("prow", "pcol"),
        P("prow", "pcol"),
        P(None, "pcol", None, None),
        P(),
    )
    return jax.shard_map(
        body,
        mesh=mesh,
        in_specs=placed,
        out_specs=(P(None, "prow", None, "pcol"), P("prow", "pcol"), P("prow", "pcol")),
        check_vma=False,
    )
```

```python
import functools

import jax
import jax.numpy as jnp
from jax import lax
from jax.experimental import pallas as pl
from jax.experimental.pallas import tpu as pltpu
from jax.sharding import PartitionSpec as P

GRID = ("prow", "pcol")
VMEM_LIMIT = 60 * 1024 * 1024


def split(value):
    high = value.astype(jnp.bfloat16)
    return high, (value - high.astype(jnp.float32)).astype(jnp.bfloat16)


def dot3(left, right):
    (lh, ll), (rh, rl) = left, right
    dot = functools.partial(jnp.dot, preferred_element_type=jnp.float32)
    return dot(lh, rh) + (dot(lh, rl) + dot(ll, rh))


PLANE, COL, PLANE0, NEWEST, MEMBER, SWAP_B, FIRST_IN, LAST_IN, LAST_LEVEL, USE_LAST, OWNS, ODD, LATE, COUNTS = range(14)


def call(kernel, info, grid, in_specs, out_specs, out_shape, scratch, args, alias=None, after=(), short=False):
    count = len(args)
    after = [a for a in after if all(a is not arg for arg in args)]

    def run(*refs):
        kernel(*refs[: count + 1], *refs[count + 1 + len(after) :])

    return pl.pallas_call(
        run,
        grid_spec=pltpu.PrefetchScalarGridSpec(
            num_scalar_prefetch=1,
            grid=grid,
            in_specs=in_specs + [pl.BlockSpec(memory_space=pl.ANY)] * len(after),
            out_specs=out_specs,
            scratch_shapes=scratch,
        ),
        out_shape=out_shape,
        input_output_aliases=alias or {},
        compiler_params=pltpu.CompilerParams(vmem_limit_bytes=VMEM_LIMIT),
        cost_estimate=pl.CostEstimate(flops=1 if short else 10**14, bytes_accessed=1, transcendentals=0),
    )(info, *args, *after)


def factor_kernel(paired, cols, info, factors, came, first, first_t, half_a, chain_b, prev, cur):
    window = first.shape[0]
    half = window // 2
    at = info[COL]
    rows = lax.broadcasted_iota(jnp.int32, (window, window), 0)
    lanes = lax.broadcasted_iota(jnp.int32, (window, window), 1)
    identity = (rows == lanes).astype(jnp.float32)
    own = jnp.where(info[COUNTS + at] > 0, factors[0, 0], identity)
    first[...] = own
    if paired:
        owner = at - lax.rem(at, 2) + info[PLANE]
        there = jnp.where(info[COUNTS + owner] > 0, came[...], identity)
        own = jnp.where(info[OWNS] == 1, own, there)
    own = own.T
    first_t[0] = own[:half]
    first_t[1] = own[half:]
    half_a[...] = jnp.where(info[MEMBER] == 1, own[half:], own[:half])
    on = (info[COUNTS + cols + at] > 0) & (at < cols - 1)
    own = jnp.where(on, factors[1, 0], identity)
    prev[...] = own[:, half:]
    cur[...] = own[:, :half]
    chain_b[...] = jnp.where(info[OWNS] == 1, own[:, :half], own[:, half:]).T


def pair_kernel(info, own, across, out):
    odd = info[ODD] == 1
    out[0] = jnp.where(odd, across[...], own[...])
    out[1] = jnp.where(odd, own[...], across[...])


def rest_kernel(info, value, out):
    del info, value, out


def first_kernel(joint, info, seg, col, near, far, prev_top, *rest):
    sends, (last_top, col_h, col_l, carry) = rest[: 2 - joint], rest[2 - joint :]
    half = prev_top.shape[0]
    i = pl.program_id(0)

    @pl.when(i == 0)
    def _():
        col_h[...], col_l[...] = split(col[...])
        carry[...] = prev_top[...]

    mid = split(dot3(split(seg[...]), (col_h[...], col_l[...])))
    out = dot3(split(jnp.concatenate([near[...], far[...]], axis=0)), mid)
    sent = jnp.where(info[PLANE0] == 1, carry[...], out[:half])
    if joint:
        sends[0][0] = out[half:]
        sends[0][1] = sent
    else:
        sends[0][...] = out[half:]
        sends[1][...] = sent
    carry[...] = out[:half]
    last_top[...] = out[:half]


def second_kernel(begin, count, tail, older, turn, info, near, far, bottom, sent, got_bottom, got_top, *rest):
    left, right = rest[-2:]
    half = bottom.shape[0]

    @pl.when(pl.program_id(0) < count)
    def _():
        a, b = near[...], far[...]
        if older:
            late = info[LATE] == 1
            a, b = jnp.where(late, rest[-4][...], a), jnp.where(late, rest[-3][...], b)
        turned = info[turn] == 1
        lower, upper = split(jnp.where(turned, b, a)), split(jnp.where(turned, a, b))

        def stacked(one, other):
            return split(jnp.concatenate([one, other], axis=0))

        new_bottom = dot3(lower, stacked(bottom[...], got_top[...]))
        new_top = dot3(upper, stacked(got_bottom[...], sent[...]))
        passing = (info[PLANE0] == 1) & (begin + pl.program_id(0) == info[NEWEST] + 1)
        new_top = jnp.where(passing, sent[...], new_top)
        left[0] = new_bottom[:, :half]
        left[1] = new_top[:, :half]
        right[0] = new_bottom[:, half:]
        right[1] = new_top[:, half:]

    if tail:

        @pl.when(pl.program_id(0) == count)
        def _():
            left[0] = left[1] = rest[0][:, :half]
            right[0] = right[1] = rest[0][:, half:]


def split_columns(prev, cur, scratch):
    prev_h, prev_l, cur_h, cur_l = scratch
    prev_h[...], prev_l[...] = split(prev[...])
    cur_h[...], cur_l[...] = split(cur[...])


def columns(left_in, mine_left, mine_right, right_in, scratch, out):
    prev_h, prev_l, cur_h, cur_l = scratch
    half = mine_left.shape[1]

    def wide(one, other):
        return split(jnp.concatenate([one, other], axis=1))

    out[:, :half] = dot3(wide(left_in, mine_left), (prev_h[...], prev_l[...]))
    out[:, half:] = dot3(wide(mine_right, right_in), (cur_h[...], cur_l[...]))


def third_kernel(begin, last_unit, slots, info, left, right, up_far, up_near, down_near, down_far, down_last, prev, cur, held, out, *scratch):
    del held
    *scratch, made, sems = scratch
    e, count = pl.program_id(0), made.shape[0]
    half = left.shape[1]

    def copies(unit):
        slot = lax.rem(info[NEWEST] - begin - unit + slots, slots)
        upper = lax.rem(slot + info[PLANE0], slots)
        for h, row in enumerate(((2 * slot + 1) * half, 2 * upper * half)):
            place = pl.ds(pl.multiple_of(row, half), half)
            yield pltpu.make_async_copy(made.at[unit, pl.ds(h * half, half)], out.at[place], sems.at[unit, h])

    @pl.when(e == 0)
    def _():
        split_columns(prev, cur, scratch)

    def flat(ref):
        return ref[...].reshape(2 * half, half)

    left_in = jnp.where(info[FIRST_IN] == 1, flat(up_far), flat(up_near))
    far = flat(down_far)
    ends_here = (info[USE_LAST] == 1) & (begin + e == last_unit)
    far = jnp.concatenate([far[:half], jnp.where(ends_here, down_last[...], far[half:])], axis=0)
    right_in = jnp.where(info[LAST_IN] == 1, far, flat(down_near))
    for unit in range(count):

        @pl.when(e == unit)
        def _():
            columns(left_in, flat(left), flat(right), right_in, scratch, made.at[unit])
            for copy in copies(unit):
                copy.start()

    @pl.when(e == count - 1)
    def _():
        for unit in range(count):
            for copy in copies(unit):
                copy.wait()


def last_kernel(info, top, up_far, up_near, down_near, prev, cur, held, out, *scratch):
    del held
    half = top.shape[0]
    split_columns(prev, cur, scratch)
    left_in = jnp.where(info[FIRST_IN] == 1, up_far[...], up_near[...])
    columns(left_in, top[:, :half], top[:, half:], down_near[...], scratch, out)

def rows_kernel(above_blocks, info, above, basis, col, left, right, col_h, col_l):
    half = left.shape[1]
    i = pl.program_id(0)

    @pl.when(i == 0)
    def _():
        col_h[...], col_l[...] = split(col[...])

    rows = jnp.where(i < above_blocks, above[...], basis[...])
    out = dot3(split(rows), (col_h[...], col_l[...]))
    left[...] = out[:, :half]
    right[...] = out[:, half:]


def rows_end_kernel(info, left, right, left_in, right_in, prev, cur, out, *scratch):
    @pl.when(pl.program_id(0) == 0)
    def _():
        split_columns(prev, cur, scratch)

    columns(left_in[...], left[...], right[...], right_in[...], scratch, out)


def whole(shape):
    return pl.BlockSpec(shape, lambda *_: (0,) * len(shape))


def body(segment, above_rows, basis_rows, factors, swap_counts):
    slots = segment.shape[0]
    window = segment.shape[2]
    half = window // 2
    planes = lax.axis_size("prow")
    cols = lax.axis_size("pcol")
    plane = lax.axis_index("prow")
    col = lax.axis_index("pcol")
    f32, bf = jnp.float32, jnp.bfloat16
    paired = planes == 2
    fold = next(size for size in (4, 2, 1) if slots % size == 0) if paired else 1
    group = planes * fold
    levels = slots // fold
    level = col // group
    newest = fold * level + fold - 1
    owner = plane if paired else (plane + planes - 1) % planes
    member = col % planes
    place = [
        plane,
        col,
        plane == 0,
        newest,
        member,
        (member != plane) & paired,
        col % group == 0,
        col % group == group - 1,
        level == levels - 1,
        (plane == 0) & (level == levels - 2),
        member == plane,
        (col // 2) % 2,
        (col // 4) % 2 == 0,
    ]
    info = jnp.concatenate([jnp.stack([jnp.asarray(v, jnp.int32) for v in place]), swap_counts.reshape(-1)])

    def send(value, route):
        return lax.ppermute(value, GRID, [(a * cols + b, c * cols + d) for (a, b), (c, d) in route])

    everyone = [(p, c) for p in range(planes) for c in range(cols)]

    def along(value, step, wanted=lambda c: True):
        route = [((p, c), (p, c + step)) for p, c in everyone if 0 <= c + step < cols and wanted(c)]
        return send(value, route)

    def shape(*dims):
        return jax.ShapeDtypeStruct(dims, f32)

    last = []

    if paired:
        raw = factors[0, 0]
        came = send(raw, [((p, c), (p, c + 1 - 2 * p)) for p, c in everyone if c % 2 == p])
    else:
        came = factors[0, 0]
    own_first, full_first, half_a, chain_b, prev_own, cur = call(
        functools.partial(factor_kernel, paired, cols),
        info,
        (1,),
        [whole((2, 1, window, window)), whole((window, window))],
        [whole((window, window)), whole((2, half, window))]
        + [whole((half, window))] * 2
        + [whole((window, half))] * 2,
        [shape(window, window), shape(2, half, window)] + [shape(half, window)] * 2 + [shape(window, half)] * 2,
        [],
        (factors, came),
    )
    last.append(own_first)
    rows = lax.broadcasted_iota(jnp.int32, (window, half), 0)
    lanes = lax.broadcasted_iota(jnp.int32, (window, half), 1)

    def hopped(value, hop):
        return along(value, group, lambda c: c // group >= hop - 1)

    def chained(value):
        values = [value]
        for hop in range(1, levels):
            values.append(hopped(values[-1], hop))
        return values

    teams = [list(range(g * group, (g + 1) * group)) for g in range(cols // group)]

    def gathered(value):
        mine = lax.all_gather(value, "pcol", axis_index_groups=teams)
        return (mine, lambda q: 2 * q, mine, lambda q: 2 * q + 1)

    def placed(value, *after):
        anywhere = pl.BlockSpec(memory_space=pl.ANY)
        value = call(
            rest_kernel, info, (1,), [anywhere], anywhere, shape(*value.shape), [], (value,), {1: 0}, [*last[-1:], *after]
        )
        last.append(value)
        return value

    def paired_up(own, across, *after):
        out = call(
            pair_kernel,
            info,
            (1,),
            [whole((half, window))] * 2,
            whole((2, half, window)),
            shape(2, half, window),
            [],
            (own, across),
            after=[*last[-1:], *after],
        )
        last.append(out)
        return out

    def with_swapped(mine):
        other = send(mine, [((p, c), (p, c + 1 - 2 * (c % 2))) for p, c in everyone])
        return (mine, lambda q: q % 2, other, lambda q: q % 2)

    if not paired:

        def shared(value, holder):
            value = jnp.where(member == holder, value, jnp.zeros_like(value))
            return lax.psum(value, "pcol", axis_index_groups=teams)

        full_first = shared(full_first, plane)
        both = jnp.stack([shared(chain_b, plane), shared(chain_b, owner)])
        first_factors = [(value, lambda q: 0, value, lambda q: 1) for value in chained(full_first)]
        second_factors = [(value, lambda q: 0, value, lambda q: 1) for value in chained(both) for _ in range(fold)]

    def previous(value):
        came_prev = along(value, 1)
        return came_prev, jnp.where(col == 0, (rows == lanes + half).astype(f32), came_prev)

    seg = segment.reshape(slots * window, window)

    def slot_of(t, f):
        return lax.rem(f[NEWEST] - t + slots, slots)

    def factor_specs(factor, at):

        def spec(array, first):
            return pl.BlockSpec((None, half, window), lambda i, f: (first(at(i)), 0, 0))

        return [spec(*factor[:2]), spec(*factor[2:])]

    def first_step(batch, prev_top, joint, after):
        count, begin = len(batch), batch[0]
        factor = first_factors[begin // fold] if begin or not paired else (full_first, lambda q: 0, full_first, lambda q: 1)
        place = 0 if begin == 0 else fold - 1 - begin % fold
        if joint:
            specs = [pl.BlockSpec((None, 2, half, window), lambda i, f: (i, 0, 0, 0))]
            shapes = [shape(count, 2, half, window)]
        else:
            specs = [pl.BlockSpec((None, None, half, window), lambda i, f: (i, 0, 0, 0))] * 2
            shapes = [shape(count, 1, half, window)] * 2
        outs = call(
            functools.partial(first_kernel, joint),
            info,
            (count,),
            [
                pl.BlockSpec((window, window), lambda i, f: (slot_of(begin + i, f), 0)),
                whole((window, window)),
                *factor_specs(factor, lambda i: place - i),
                whole((half, window)),
            ],
            specs + [whole((half, window))],
            shapes + [shape(half, window)],
            [pltpu.VMEM((window, window), bf)] * 2 + [pltpu.VMEM((half, window), f32)],
            (seg, own_first, factor[0], factor[2], prev_top),
            after=[*last[-1:], *after],
        )
        return outs[:-1], outs[-1]

    def exchange(batch, sends):
        down, up = [], []
        for p, c in everyone:
            places = [fold * (c // group) + fold - 1 - t for t in batch]
            tiles = [at * planes + p for at in places if at >= 0]
            if any(tile <= c and tile < cols - 1 for tile in tiles):
                down.append(((p, c), ((p + 1) % planes, c)))
            if any((tile if p else tile + planes) <= c for tile in tiles):
                up.append(((p, c), ((p - 1) % planes, c)))
        if len(sends) == 1:
            return [send(sends[0], sorted(set(down + up)))]
        return [send(sends[0], down), send(sends[1], up)]

    def second_step(batch, size, at, sends, gots, held, ended, after):
        count, begin = len(batch), batch[0]
        factor, place = second_factors[begin], fold - 1 - begin % fold
        older = second_factors[begin - 2] if by_level and begin == 2 else ()
        turn = PLANE if paired and not (by_level and begin < fold) else SWAP_B
        specs = lambda factor: factor_specs(factor, lambda i: place - inner(i)) if factor else []
        inner = lambda i: jnp.minimum(i, count - 1)
        piece = lambda k: pl.BlockSpec((None, None, half, window), lambda i, f: (inner(i), k, 0, 0))
        pieces = [piece(0), piece(len(sends) % 2)]
        ends = [pl.BlockSpec((2, half, half), lambda i, f: (at + i, 0, 0))] * 2
        extra = [whole((half, window))] if ended else [pl.BlockSpec(memory_space=pl.ANY)] * len(held)
        return call(
            functools.partial(second_kernel, begin, count, bool(ended), bool(older), turn),
            info,
            (count + len(ended),),
            specs(factor) + pieces + pieces + extra + specs(older),
            ends,
            [shape(2 * size, half, half)] * 2,
            [],
            (factor[0], factor[2], sends[0], sends[-1], gots[0], gots[-1], *ended, *held, *older[::2]),
            {7 + k: k for k in range(len(held))},
            [*last[-1:], *after],
        )

    split_scratch = [pltpu.VMEM((window, half), bf)] * 4

    counts = (above_rows.shape[0], basis_rows.shape[0])
    deep = window if all(n % window == 0 for n in counts) else half
    above_blocks, basis_blocks = (n // deep for n in counts)

    def rows_step(after=()):
        tall = pl.BlockSpec((deep, half), lambda i, f: (i, 0))
        blocks = above_blocks + basis_blocks
        return call(
            functools.partial(rows_kernel, above_blocks),
            info,
            (blocks,),
            [
                pl.BlockSpec((deep, window), lambda i, f: (jnp.minimum(i, above_blocks - 1), 0)),
                pl.BlockSpec((deep, window), lambda i, f: (jnp.maximum(i - above_blocks, 0), 0)),
                whole((window, window)),
            ],
            [tall] * 2,
            [shape(blocks * deep, half)] * 2,
            [pltpu.VMEM((window, window), bf)] * 2,
            (above_rows, basis_rows, own_first),
            after=[*last[-1:], *after],
        )

    def rows_end(first, blocks, parts, after):
        tall = pl.BlockSpec((deep, half), lambda i, f: (first + i, 0))
        return call(
            rows_end_kernel,
            info,
            (blocks,),
            [tall] * 4 + [whole((window, half))] * 2,
            pl.BlockSpec((deep, window), lambda i, f: (i, 0)),
            shape(blocks * deep, window),
            split_scratch,
            (*parts, prev, cur),
            after=[*last[-1:], *after],
        )

    lefts, rights, ups, downs = ([None] * slots for _ in range(4))

    def third_step(batch, held, after):
        begin = batch[0]
        fresh = held is None
        parts = [lefts[begin], rights[begin]]
        parts.append(ups[begin - fold] if begin >= fold else (no_strips, 0))
        parts += [ups[begin], downs[begin], downs[(begin + fold) % slots]]
        piece = lambda at: pl.BlockSpec((2, half, half), lambda e, f: (at + e, 0, 0))
        args = [array for array, _ in parts]
        ending = slots - fold in batch
        tail_row = 2 * ending_strips[2] if ending else 0
        return call(
            functools.partial(third_kernel, begin, slots - fold, slots),
            info,
            (len(batch),),
            [piece(at) for _, at in parts]
            + [pl.BlockSpec((None, half, half), lambda e, f: (tail_row, 0, 0))]
            + [whole((window, half))] * 2
            + [pl.BlockSpec(memory_space=pl.ANY)],
            pl.BlockSpec(memory_space=pl.ANY),
            shape(*seg.shape),
            split_scratch
            + [pltpu.VMEM((len(batch), window, window), f32), pltpu.SemaphoreType.DMA((len(batch), 2))],
            (*args, ending_strips[1] if ending else args[0], prev, cur, args[0] if fresh else held),
            None if fresh else {10: 0},
            [*last[-1:], *after],
        )

    def last_step(held):
        quarter = lambda at: pl.BlockSpec((None, half, half), lambda i, f: (at, 0, 0))
        array, at = ups[slots - fold]

        def out_block(i, f):
            return (jnp.where((f[LAST_LEVEL] == 1) & (f[PLANE0] == 1), 0, 2 * slot_of(slots - 1, f) + 1), 0)

        return call(
            last_kernel,
            info,
            (1,),
            [whole((half, window)), quarter(2 * at + 1)] + [quarter(2 * ending_strips[2])] * 2
            + [whole((window, half))] * 2
            + [pl.BlockSpec(memory_space=pl.ANY)],
            pl.BlockSpec((half, window), out_block),
            shape(*seg.shape),
            split_scratch,
            (tops[-1], array, *ending_strips[:2], prev, cur, held),
            {7: 0},
            last[-1:],
        )

    tops, sent, got, made = [jnp.zeros((half, window), f32)], {}, {}, {}
    no_strips = jnp.zeros((2 * slots, half, half), f32)

    def do_first(batch, after=()):
        sent[batch[0]], top = first_step(batch, tops[-1], paired, after)
        tops.append(top)
        last.append(top)
        got[batch[0]] = exchange(batch, sent[batch[0]])

    def do_second(batch, strip, ended=(), after=()):
        begin = batch[0]
        held = made.get(strip[0], ())
        made[strip[0]] = second_step(
            batch, len(strip) + len(ended), begin - strip[0], sent[begin], got[begin], held, ended, after
        )
        last.append(made[strip[0]][0])
        if batch[-1] == strip[-1]:
            left, right = made[strip[0]]


            def filled(c):
                first = fold * (c // group) + fold - 1
                return any(-1 <= first - t <= c // planes for t in strip)

            up, down = along(right, 1, filled), along(left, -1, filled)
            for place, t in enumerate(strip):
                lefts[t], rights[t] = (left, place), (right, place)
                ups[t], downs[t] = (up, place), (down, place)
            return up, down, len(strip)

    out = [None]

    def do_third(batch, after=()):
        out[0] = third_step(batch, out[0], after)
        last.append(out[0])

    def do_last():
        out[0] = last_step(out[0])
        last.append(out[0])

    def do_rows(after=()):
        left, right = rows_step(after)
        last.append(left)
        return left, right, along(right, 1), along(left, -1)

    def do_rows_end(which, after=()):
        first, blocks = ((0, above_blocks), (above_blocks, basis_blocks))[which]
        row_ends.append(rows_end(first, blocks, parts, after))
        last.append(row_ends[-1])

    row_ends = []
    def hop(value, distance):
        return along(value, group // 2, lambda c: c // (group // 2) >= distance - 1)

    by_level = paired and fold == 4 and levels == 2
    if by_level:
        first_factors = [gathered(half_a)]
        hop_a = hopped(half_a, 1)
        across = send(chain_b, [((p, c), (p, c // 4 * 4 + (c + 2) % 4)) for p, c in everyone])
        do_first([0])
        came_prev, prev = previous(prev_own)
        pieces = paired_up(chain_b, across, came_prev)
        second_factors = [with_swapped(pieces)] * 2
        pieces = hop(pieces, 1)
        do_first([1], got[0])
        first_factors.append(gathered(placed(hop_a)))
        do_first([2, 3], [second_factors[0][2]])
        second_factors += [with_swapped(placed(pieces))] * 2
        hop_b = hopped(placed(chain_b), 1)
        do_second([0], [0, 1, 2, 3], after=got[1])
        parts = do_rows([second_factors[2][2]])
        do_second([1], [0, 1, 2, 3])
        do_first([4, 5], got[2])
        second_factors += [gathered(placed(hop_b))] * fold
        do_second([2, 3], [0, 1, 2, 3], after=parts[2:3])
        do_first([6, 7], parts[3:])
        do_rows_end(0)
        do_rows_end(1)
        got[4] = [placed(got[4][0])]
        ending_strips = do_second([4, 5], [4, 5], ended=[tops[-1]])
        do_second([6, 7], [6, 7], after=[ups[0][0], downs[0][0]])
        do_third([0, 1])
        do_third([4, 5])
        do_last()
        do_third([2, 3])
        do_third([6, 7])
    else:
        _, prev = previous(prev_own)
        parts = do_rows()
        if paired:
            first_factors = [gathered(value) for value in chained(half_a)]
            second_factors = [gathered(value) for value in chained(chain_b) for _ in range(fold)]
        for t in range(slots):
            do_first([t])
        for t in range(slots):
            ending_strips = do_second([t], [t], ended=[tops[-1]] if t == slots - 1 else ())
        for t in range(slots - 1):
            do_third([t])
        do_last()
        do_third([slots - 1])
        do_rows_end(0)
        do_rows_end(1)
    return (out[0].reshape(segment.shape), *row_ends)


def solution(mesh):
    placed = (
        P(None, "prow", None, "pcol"),
        P("prow", "pcol"),
        P("prow", "pcol"),
        P(None, "pcol", None, None),
        P(),
    )
    return jax.shard_map(
        body,
        mesh=mesh,
        in_specs=placed,
        out_specs=(P(None, "prow", None, "pcol"), P("prow", "pcol"), P("prow", "pcol")),
        check_vma=False,
    )
```

```python
import functools

import jax
import jax.numpy as jnp
from jax import lax
from jax.experimental import pallas as pl
from jax.experimental.pallas import tpu as pltpu
from jax.sharding import PartitionSpec as P

GRID = ("prow", "pcol")
VMEM_LIMIT = 60 * 1024 * 1024


def split(value):
    high = value.astype(jnp.bfloat16)
    return high, (value - high.astype(jnp.float32)).astype(jnp.bfloat16)


def dot3(left, right):
    (lh, ll), (rh, rl) = left, right
    dot = functools.partial(jnp.dot, preferred_element_type=jnp.float32)
    return dot(lh, rh) + (dot(lh, rl) + dot(ll, rh))


PLANE, COL, PLANE0, NEWEST, MEMBER, SWAP_B, FIRST_IN, LAST_IN, LAST_LEVEL, USE_LAST, OWNS, ODD, LATE, COUNTS = range(14)


def call(kernel, info, grid, in_specs, out_specs, out_shape, scratch, args, alias=None, after=(), short=False):
    count = len(args)
    after = [a for a in after if all(a is not arg for arg in args)]

    def run(*refs):
        kernel(*refs[: count + 1], *refs[count + 1 + len(after) :])

    return pl.pallas_call(
        run,
        grid_spec=pltpu.PrefetchScalarGridSpec(
            num_scalar_prefetch=1,
            grid=grid,
            in_specs=in_specs + [pl.BlockSpec(memory_space=pl.ANY)] * len(after),
            out_specs=out_specs,
            scratch_shapes=scratch,
        ),
        out_shape=out_shape,
        input_output_aliases=alias or {},
        compiler_params=pltpu.CompilerParams(vmem_limit_bytes=VMEM_LIMIT),
        cost_estimate=pl.CostEstimate(flops=1 if short else 10**14, bytes_accessed=1, transcendentals=0),
    )(info, *args, *after)


def factor_kernel(paired, cols, info, factors, came, first, first_t, half_a, chain_b, prev, cur):
    window = first.shape[0]
    half = window // 2
    at = info[COL]
    rows = lax.broadcasted_iota(jnp.int32, (window, window), 0)
    lanes = lax.broadcasted_iota(jnp.int32, (window, window), 1)
    identity = (rows == lanes).astype(jnp.float32)
    own = jnp.where(info[COUNTS + at] > 0, factors[0, 0], identity)
    first[...] = own
    if paired:
        owner = at - lax.rem(at, 2) + info[PLANE]
        there = jnp.where(info[COUNTS + owner] > 0, came[...], identity)
        own = jnp.where(info[OWNS] == 1, own, there)
    own = own.T
    first_t[0] = own[:half]
    first_t[1] = own[half:]
    half_a[...] = jnp.where(info[MEMBER] == 1, own[half:], own[:half])
    on = (info[COUNTS + cols + at] > 0) & (at < cols - 1)
    own = jnp.where(on, factors[1, 0], identity)
    prev[...] = own[:, half:]
    cur[...] = own[:, :half]
    chain_b[...] = jnp.where(info[OWNS] == 1, own[:, :half], own[:, half:]).T


def pair_kernel(info, own, across, out):
    odd = info[ODD] == 1
    out[0] = jnp.where(odd, across[...], own[...])
    out[1] = jnp.where(odd, own[...], across[...])


def rest_kernel(info, value, out):
    del info, value, out


def first_kernel(joint, info, seg, col, near, far, prev_top, *rest):
    sends, (last_top, col_h, col_l, carry) = rest[: 2 - joint], rest[2 - joint :]
    half = prev_top.shape[0]
    i = pl.program_id(0)

    @pl.when(i == 0)
    def _():
        col_h[...], col_l[...] = split(col[...])
        carry[...] = prev_top[...]

    mid = split(dot3(split(seg[...]), (col_h[...], col_l[...])))
    out = dot3(split(jnp.concatenate([near[...], far[...]], axis=0)), mid)
    sent = jnp.where(info[PLANE0] == 1, carry[...], out[:half])
    if joint:
        sends[0][0] = out[half:]
        sends[0][1] = sent
    else:
        sends[0][...] = out[half:]
        sends[1][...] = sent
    carry[...] = out[:half]
    last_top[...] = out[:half]


def second_kernel(begin, count, tail, older, turn, info, near, far, bottom, sent, got_bottom, got_top, *rest):
    left, right = rest[-2:]
    half = bottom.shape[0]

    @pl.when(pl.program_id(0) < count)
    def _():
        a, b = near[...], far[...]
        if older:
            late = info[LATE] == 1
            a, b = jnp.where(late, rest[-4][...], a), jnp.where(late, rest[-3][...], b)
        turned = info[turn] == 1
        lower, upper = split(jnp.where(turned, b, a)), split(jnp.where(turned, a, b))

        def stacked(one, other):
            return split(jnp.concatenate([one, other], axis=0))

        new_bottom = dot3(lower, stacked(bottom[...], got_top[...]))
        new_top = dot3(upper, stacked(got_bottom[...], sent[...]))
        passing = (info[PLANE0] == 1) & (begin + pl.program_id(0) == info[NEWEST] + 1)
        new_top = jnp.where(passing, sent[...], new_top)
        left[0] = new_bottom[:, :half]
        left[1] = new_top[:, :half]
        right[0] = new_bottom[:, half:]
        right[1] = new_top[:, half:]

    if tail:

        @pl.when(pl.program_id(0) == count)
        def _():
            left[0] = left[1] = rest[0][:, :half]
            right[0] = right[1] = rest[0][:, half:]


def split_columns(prev, cur, scratch):
    prev_h, prev_l, cur_h, cur_l = scratch
    prev_h[...], prev_l[...] = split(prev[...])
    cur_h[...], cur_l[...] = split(cur[...])


def columns(left_in, mine_left, mine_right, right_in, scratch, out):
    prev_h, prev_l, cur_h, cur_l = scratch
    half = mine_left.shape[1]

    def wide(one, other):
        return split(jnp.concatenate([one, other], axis=1))

    out[:, :half] = dot3(wide(left_in, mine_left), (prev_h[...], prev_l[...]))
    out[:, half:] = dot3(wide(mine_right, right_in), (cur_h[...], cur_l[...]))


def third_kernel(begin, last_unit, slots, none_far, again, info, left, right, up_far, up_near, down_near, down_far, down_last, prev, cur, held, out, *scratch):
    del held
    wanted = (info[LAST_IN] == 1) | (not again)
    *scratch, made, sems = scratch
    e, count = pl.program_id(0), made.shape[0]
    half = left.shape[1]

    def copies(unit):
        slot = lax.rem(info[NEWEST] - begin - unit + slots, slots)
        upper = lax.rem(slot + info[PLANE0], slots)
        for h, row in enumerate(((2 * slot + 1) * half, 2 * upper * half)):
            place = pl.ds(pl.multiple_of(row, half), half)
            yield pltpu.make_async_copy(made.at[unit, pl.ds(h * half, half)], out.at[place], sems.at[unit, h])

    @pl.when(e == 0)
    def _():
        split_columns(prev, cur, scratch)

    def flat(ref):
        return ref[...].reshape(2 * half, half)

    before = jnp.zeros((2 * half, half), jnp.float32) if none_far else flat(up_far)
    left_in = jnp.where(info[FIRST_IN] == 1, before, flat(up_near))
    far = flat(down_far)
    ends_here = (info[USE_LAST] == 1) & (begin + e == last_unit)
    far = jnp.concatenate([far[:half], jnp.where(ends_here, down_last[...], far[half:])], axis=0)
    right_in = jnp.where(info[LAST_IN] == 1, far, flat(down_near))
    for unit in range(count):

        @pl.when((e == unit) & wanted)
        def _():
            columns(left_in, flat(left), flat(right), right_in, scratch, made.at[unit])
            for copy in copies(unit):
                copy.start()

    @pl.when((e == count - 1) & wanted)
    def _():
        for unit in range(count):
            for copy in copies(unit):
                copy.wait()


def last_kernel(info, top, up_far, up_near, down_near, prev, cur, held, out, *scratch):
    del held
    half = top.shape[0]
    split_columns(prev, cur, scratch)
    left_in = jnp.where(info[FIRST_IN] == 1, up_far[...], up_near[...])
    columns(left_in, top[:, :half], top[:, half:], down_near[...], scratch, out)

def rows_kernel(above_blocks, info, above, basis, col, left, right, col_h, col_l):
    half = left.shape[1]
    i = pl.program_id(0)

    @pl.when(i == 0)
    def _():
        col_h[...], col_l[...] = split(col[...])

    rows = jnp.where(i < above_blocks, above[...], basis[...])
    out = dot3(split(rows), (col_h[...], col_l[...]))
    left[...] = out[:, :half]
    right[...] = out[:, half:]


def rows_end_kernel(info, left, right, left_in, right_in, prev, cur, out, *scratch):
    @pl.when(pl.program_id(0) == 0)
    def _():
        split_columns(prev, cur, scratch)

    columns(left_in[...], left[...], right[...], right_in[...], scratch, out)


def whole(shape):
    return pl.BlockSpec(shape, lambda *_: (0,) * len(shape))


def body(segment, above_rows, basis_rows, factors, swap_counts):
    slots = segment.shape[0]
    window = segment.shape[2]
    half = window // 2
    planes = lax.axis_size("prow")
    cols = lax.axis_size("pcol")
    plane = lax.axis_index("prow")
    col = lax.axis_index("pcol")
    f32, bf = jnp.float32, jnp.bfloat16
    paired = planes == 2
    fold = next(size for size in (4, 2, 1) if slots % size == 0) if paired else 1
    group = planes * fold
    levels = slots // fold
    level = col // group
    newest = fold * level + fold - 1
    owner = plane if paired else (plane + planes - 1) % planes
    member = col % planes
    place = [
        plane,
        col,
        plane == 0,
        newest,
        member,
        (member != plane) & paired,
        col % group == 0,
        col % group == group - 1,
        level == levels - 1,
        (plane == 0) & (level == levels - 2),
        member == plane,
        (col // 2) % 2,
        (col // 4) % 2 == 0,
    ]
    info = jnp.concatenate([jnp.stack([jnp.asarray(v, jnp.int32) for v in place]), swap_counts.reshape(-1)])

    def send(value, route):
        return lax.ppermute(value, GRID, [(a * cols + b, c * cols + d) for (a, b), (c, d) in route])

    everyone = [(p, c) for p in range(planes) for c in range(cols)]

    def along(value, step, wanted=lambda c: True):
        route = [((p, c), (p, c + step)) for p, c in everyone if 0 <= c + step < cols and wanted(c)]
        return send(value, route)

    def shape(*dims):
        return jax.ShapeDtypeStruct(dims, f32)

    last = []

    if paired:
        raw = factors[0, 0]
        came = send(raw, [((p, c), (p, c + 1 - 2 * p)) for p, c in everyone if c % 2 == p])
    else:
        came = factors[0, 0]
    own_first, full_first, half_a, chain_b, prev_own, cur = call(
        functools.partial(factor_kernel, paired, cols),
        info,
        (1,),
        [whole((2, 1, window, window)), whole((window, window))],
        [whole((window, window)), whole((2, half, window))]
        + [whole((half, window))] * 2
        + [whole((window, half))] * 2,
        [shape(window, window), shape(2, half, window)] + [shape(half, window)] * 2 + [shape(window, half)] * 2,
        [],
        (factors, came),
    )
    last.append(own_first)
    rows = lax.broadcasted_iota(jnp.int32, (window, half), 0)
    lanes = lax.broadcasted_iota(jnp.int32, (window, half), 1)

    def hopped(value, hop):
        return along(value, group, lambda c: c // group >= hop - 1)

    def chained(value):
        values = [value]
        for hop in range(1, levels):
            values.append(hopped(values[-1], hop))
        return values

    teams = [list(range(g * group, (g + 1) * group)) for g in range(cols // group)]

    def gathered(value):
        mine = lax.all_gather(value, "pcol", axis_index_groups=teams)
        return (mine, lambda q: 2 * q, mine, lambda q: 2 * q + 1)

    def placed(value, *after):
        anywhere = pl.BlockSpec(memory_space=pl.ANY)
        value = call(
            rest_kernel, info, (1,), [anywhere], anywhere, shape(*value.shape), [], (value,), {1: 0}, [*last[-1:], *after]
        )
        last.append(value)
        return value

    def paired_up(own, across, *after):
        out = call(
            pair_kernel,
            info,
            (1,),
            [whole((half, window))] * 2,
            whole((2, half, window)),
            shape(2, half, window),
            [],
            (own, across),
            after=[*last[-1:], *after],
        )
        last.append(out)
        return out

    def with_swapped(mine):
        other = send(mine, [((p, c), (p, c + 1 - 2 * (c % 2))) for p, c in everyone])
        return (mine, lambda q: q % 2, other, lambda q: q % 2)

    if not paired:

        def shared(value, holder):
            value = jnp.where(member == holder, value, jnp.zeros_like(value))
            return lax.psum(value, "pcol", axis_index_groups=teams)

        full_first = shared(full_first, plane)
        both = jnp.stack([shared(chain_b, plane), shared(chain_b, owner)])
        first_factors = [(value, lambda q: 0, value, lambda q: 1) for value in chained(full_first)]
        second_factors = [(value, lambda q: 0, value, lambda q: 1) for value in chained(both) for _ in range(fold)]

    def previous(value):
        came_prev = along(value, 1)
        return came_prev, jnp.where(col == 0, (rows == lanes + half).astype(f32), came_prev)

    seg = segment.reshape(slots * window, window)

    def slot_of(t, f):
        return lax.rem(f[NEWEST] - t + slots, slots)

    def factor_specs(factor, at):

        def spec(array, first):
            return pl.BlockSpec((None, half, window), lambda i, f: (first(at(i)), 0, 0))

        return [spec(*factor[:2]), spec(*factor[2:])]

    def first_step(batch, prev_top, joint, after):
        count, begin = len(batch), batch[0]
        factor = first_factors[begin // fold] if begin or not paired else (full_first, lambda q: 0, full_first, lambda q: 1)
        place = 0 if begin == 0 else fold - 1 - begin % fold
        if joint:
            specs = [pl.BlockSpec((None, 2, half, window), lambda i, f: (i, 0, 0, 0))]
            shapes = [shape(count, 2, half, window)]
        else:
            specs = [pl.BlockSpec((None, None, half, window), lambda i, f: (i, 0, 0, 0))] * 2
            shapes = [shape(count, 1, half, window)] * 2
        outs = call(
            functools.partial(first_kernel, joint),
            info,
            (count,),
            [
                pl.BlockSpec((window, window), lambda i, f: (slot_of(begin + i, f), 0)),
                whole((window, window)),
                *factor_specs(factor, lambda i: place - i),
                whole((half, window)),
            ],
            specs + [whole((half, window))],
            shapes + [shape(half, window)],
            [pltpu.VMEM((window, window), bf)] * 2 + [pltpu.VMEM((half, window), f32)],
            (seg, own_first, factor[0], factor[2], prev_top),
            after=[*last[-1:], *after],
        )
        return outs[:-1], outs[-1]

    def exchange(batch, sends):
        down, up = [], []
        for p, c in everyone:
            places = [fold * (c // group) + fold - 1 - t for t in batch]
            tiles = [at * planes + p for at in places if at >= 0]
            if any(tile <= c and tile < cols - 1 for tile in tiles):
                down.append(((p, c), ((p + 1) % planes, c)))
            if any((tile if p else tile + planes) <= c for tile in tiles):
                up.append(((p, c), ((p - 1) % planes, c)))
        if len(sends) == 1:
            return [send(sends[0], sorted(set(down + up)))]
        return [send(sends[0], down), send(sends[1], up)]

    def second_step(batch, size, at, sends, gots, held, ended, after):
        count, begin = len(batch), batch[0]
        factor, place = second_factors[begin], fold - 1 - begin % fold
        older = second_factors[begin - 2] if by_level and begin == 2 else ()
        turn = PLANE if paired and not (by_level and begin < fold) else SWAP_B
        specs = lambda factor: factor_specs(factor, lambda i: place - inner(i)) if factor else []
        inner = lambda i: jnp.minimum(i, count - 1)
        piece = lambda k: pl.BlockSpec((None, None, half, window), lambda i, f: (inner(i), k, 0, 0))
        pieces = [piece(0), piece(len(sends) % 2)]
        ends = [pl.BlockSpec((2, half, half), lambda i, f: (at + i, 0, 0))] * 2
        extra = [whole((half, window))] if ended else [pl.BlockSpec(memory_space=pl.ANY)] * len(held)
        return call(
            functools.partial(second_kernel, begin, count, bool(ended), bool(older), turn),
            info,
            (count + len(ended),),
            specs(factor) + pieces + pieces + extra + specs(older),
            ends,
            [shape(2 * size, half, half)] * 2,
            [],
            (factor[0], factor[2], sends[0], sends[-1], gots[0], gots[-1], *ended, *held, *older[::2]),
            {7 + k: k for k in range(len(held))},
            [*last[-1:], *after],
        )

    split_scratch = [pltpu.VMEM((window, half), bf)] * 4

    counts = (above_rows.shape[0], basis_rows.shape[0])
    deep = window if all(n % window == 0 for n in counts) else half
    above_blocks, basis_blocks = (n // deep for n in counts)

    def rows_step(after=()):
        tall = pl.BlockSpec((deep, half), lambda i, f: (i, 0))
        blocks = above_blocks + basis_blocks
        return call(
            functools.partial(rows_kernel, above_blocks),
            info,
            (blocks,),
            [
                pl.BlockSpec((deep, window), lambda i, f: (jnp.minimum(i, above_blocks - 1), 0)),
                pl.BlockSpec((deep, window), lambda i, f: (jnp.maximum(i - above_blocks, 0), 0)),
                whole((window, window)),
            ],
            [tall] * 2,
            [shape(blocks * deep, half)] * 2,
            [pltpu.VMEM((window, window), bf)] * 2,
            (above_rows, basis_rows, own_first),
            after=[*last[-1:], *after],
        )

    def rows_end(first, blocks, parts, after):
        tall = pl.BlockSpec((deep, half), lambda i, f: (first + i, 0))
        return call(
            rows_end_kernel,
            info,
            (blocks,),
            [tall] * 4 + [whole((window, half))] * 2,
            pl.BlockSpec((deep, window), lambda i, f: (i, 0)),
            shape(blocks * deep, window),
            split_scratch,
            (*parts, prev, cur),
            after=[*last[-1:], *after],
        )

    lefts, rights, ups, downs = ([None] * slots for _ in range(4))

    def third_step(batch, held, after, early, again):
        begin = batch[0]
        fresh = held is None
        parts = [lefts[begin], rights[begin]]
        parts.append(ups[begin - fold] if begin >= fold else ups[begin])
        parts += [ups[begin], downs[begin], downs[begin if early else (begin + fold) % slots]]
        step = lambda e, f: e * f[LAST_IN] if again else e
        piece = lambda at: pl.BlockSpec((2, half, half), lambda e, f: (at + step(e, f), 0, 0))
        args = [array for array, _ in parts]
        ending = slots - fold in batch
        tail_row = 2 * ending_strips[2] if ending else 0
        return call(
            functools.partial(third_kernel, begin, slots - fold, slots, begin < fold, again),
            info,
            (len(batch),),
            [piece(at) for _, at in parts]
            + [pl.BlockSpec((None, half, half), lambda e, f: (tail_row, 0, 0))]
            + [whole((window, half))] * 2
            + [pl.BlockSpec(memory_space=pl.ANY)],
            pl.BlockSpec(memory_space=pl.ANY),
            shape(*seg.shape),
            split_scratch
            + [pltpu.VMEM((len(batch), window, window), f32), pltpu.SemaphoreType.DMA((len(batch), 2))],
            (*args, ending_strips[1] if ending else args[0], prev, cur, args[0] if fresh else held),
            None if fresh else {10: 0},
            [*last[-1:], *after],
        )

    def last_step(held):
        quarter = lambda at: pl.BlockSpec((None, half, half), lambda i, f: (at, 0, 0))
        array, at = ups[slots - fold]

        def out_block(i, f):
            return (jnp.where((f[LAST_LEVEL] == 1) & (f[PLANE0] == 1), 0, 2 * slot_of(slots - 1, f) + 1), 0)

        return call(
            last_kernel,
            info,
            (1,),
            [whole((half, window)), quarter(2 * at + 1)] + [quarter(2 * ending_strips[2])] * 2
            + [whole((window, half))] * 2
            + [pl.BlockSpec(memory_space=pl.ANY)],
            pl.BlockSpec((half, window), out_block),
            shape(*seg.shape),
            split_scratch,
            (tops[-1], array, *ending_strips[:2], prev, cur, held),
            {7: 0},
            last[-1:],
        )

    tops, sent, got, made = [jnp.zeros((half, window), f32)], {}, {}, {}

    def do_first(batch, after=()):
        sent[batch[0]], top = first_step(batch, tops[-1], paired, after)
        tops.append(top)
        last.append(top)
        got[batch[0]] = exchange(batch, sent[batch[0]])

    def do_second(batch, strip, ended=(), after=()):
        begin = batch[0]
        held = made.get(strip[0], ())
        made[strip[0]] = second_step(
            batch, len(strip) + len(ended), begin - strip[0], sent[begin], got[begin], held, ended, after
        )
        last.append(made[strip[0]][0])
        if batch[-1] == strip[-1]:
            left, right = made[strip[0]]


            def filled(c):
                first = fold * (c // group) + fold - 1
                return any(-1 <= first - t <= c // planes for t in strip)

            up, down = along(right, 1, filled), along(left, -1, filled)
            for place, t in enumerate(strip):
                lefts[t], rights[t] = (left, place), (right, place)
                ups[t], downs[t] = (up, place), (down, place)
            return up, down, len(strip)

    out = [None]

    def do_third(batch, early=False, again=False):
        out[0] = third_step(batch, out[0], (), early, again)
        last.append(out[0])

    def do_last():
        out[0] = last_step(out[0])
        last.append(out[0])

    def do_rows(after=()):
        left, right = rows_step(after)
        last.append(left)
        return left, right, along(right, 1), along(left, -1)

    def do_rows_end(which, after=()):
        first, blocks = ((0, above_blocks), (above_blocks, basis_blocks))[which]
        row_ends.append(rows_end(first, blocks, parts, after))
        last.append(row_ends[-1])

    row_ends = []
    def hop(value, distance):
        return along(value, group // 2, lambda c: c // (group // 2) >= distance - 1)

    by_level = paired and fold == 4 and levels == 2
    if by_level:
        first_factors = [gathered(half_a)]
        hop_a = hopped(half_a, 1)
        across = send(chain_b, [((p, c), (p, c // 4 * 4 + (c + 2) % 4)) for p, c in everyone])
        do_first([0])
        came_prev, prev = previous(prev_own)
        pieces = paired_up(chain_b, across, came_prev)
        second_factors = [with_swapped(pieces)] * 2
        pieces = hop(pieces, 1)
        do_first([1], got[0])
        first_factors.append(gathered(placed(hop_a)))
        do_first([2, 3], [second_factors[0][2]])
        second_factors += [with_swapped(placed(pieces))] * 2
        hop_b = hopped(placed(chain_b), 1)
        do_second([0], [0, 1, 2, 3], after=got[1])
        parts = do_rows([second_factors[2][2]])
        do_second([1], [0, 1, 2, 3])
        do_first([4, 5], got[2])
        second_factors += [gathered(placed(hop_b))] * fold
        do_second([2, 3], [0, 1, 2, 3], after=parts[2:3])
        do_first([6, 7], parts[3:])
        do_rows_end(0)
        do_rows_end(1)
        got[4] = [placed(got[4][0])]
        ending_strips = do_second([4, 5], [4, 5], ended=[tops[-1]])
        do_third([0, 1], early=True)
        do_second([6, 7], [6, 7])
        do_third([2, 3], early=True)
        do_third([4, 5])
        do_third([0, 1], again=True)
        do_last()
        do_third([6, 7])
        do_third([2, 3], again=True)
    else:
        _, prev = previous(prev_own)
        parts = do_rows()
        if paired:
            first_factors = [gathered(value) for value in chained(half_a)]
            second_factors = [gathered(value) for value in chained(chain_b) for _ in range(fold)]
        for t in range(slots):
            do_first([t])
        for t in range(slots):
            ending_strips = do_second([t], [t], ended=[tops[-1]] if t == slots - 1 else ())
        for t in range(slots - 1):
            do_third([t])
        do_last()
        do_third([slots - 1])
        do_rows_end(0)
        do_rows_end(1)
    return (out[0].reshape(segment.shape), *row_ends)


def solution(mesh):
    placed = (
        P(None, "prow", None, "pcol"),
        P("prow", "pcol"),
        P("prow", "pcol"),
        P(None, "pcol", None, None),
        P(),
    )
    return jax.shard_map(
        body,
        mesh=mesh,
        in_specs=placed,
        out_specs=(P(None, "prow", None, "pcol"), P("prow", "pcol"), P("prow", "pcol")),
        check_vma=False,
    )
```

```python
import functools

import jax
import jax.numpy as jnp
from jax import lax
from jax.experimental import pallas as pl
from jax.experimental.pallas import tpu as pltpu
from jax.sharding import PartitionSpec as P

GRID = ("prow", "pcol")
VMEM_LIMIT = 60 * 1024 * 1024


def split(value):
    high = value.astype(jnp.bfloat16)
    return high, (value - high.astype(jnp.float32)).astype(jnp.bfloat16)


def dot3(left, right):
    (lh, ll), (rh, rl) = left, right
    dot = functools.partial(jnp.dot, preferred_element_type=jnp.float32)
    return dot(lh, rh) + (dot(lh, rl) + dot(ll, rh))


PLANE, COL, PLANE0, NEWEST, MEMBER, SWAP_B, FIRST_IN, LAST_IN, LAST_LEVEL, USE_LAST, OWNS, ODD, LATE, COUNTS = range(14)


def call(kernel, info, grid, in_specs, out_specs, out_shape, scratch, args, alias=None, after=(), short=False):
    count = len(args)
    after = [a for a in after if all(a is not arg for arg in args)]

    def run(*refs):
        kernel(*refs[: count + 1], *refs[count + 1 + len(after) :])

    return pl.pallas_call(
        run,
        grid_spec=pltpu.PrefetchScalarGridSpec(
            num_scalar_prefetch=1,
            grid=grid,
            in_specs=in_specs + [pl.BlockSpec(memory_space=pl.ANY)] * len(after),
            out_specs=out_specs,
            scratch_shapes=scratch,
        ),
        out_shape=out_shape,
        input_output_aliases=alias or {},
        compiler_params=pltpu.CompilerParams(vmem_limit_bytes=VMEM_LIMIT),
        cost_estimate=pl.CostEstimate(flops=1 if short else 10**14, bytes_accessed=1, transcendentals=0),
    )(info, *args, *after)


def factor_kernel(paired, cols, info, factors, came, first, first_t, half_a, chain_b, prev, cur):
    window = first.shape[0]
    half = window // 2
    at = info[COL]
    rows = lax.broadcasted_iota(jnp.int32, (window, window), 0)
    lanes = lax.broadcasted_iota(jnp.int32, (window, window), 1)
    identity = (rows == lanes).astype(jnp.float32)
    own = jnp.where(info[COUNTS + at] > 0, factors[0, 0], identity)
    first[...] = own
    if paired:
        owner = at - lax.rem(at, 2) + info[PLANE]
        there = jnp.where(info[COUNTS + owner] > 0, came[...], identity)
        own = jnp.where(info[OWNS] == 1, own, there)
    own = own.T
    first_t[0] = own[:half]
    first_t[1] = own[half:]
    half_a[...] = jnp.where(info[MEMBER] == 1, own[half:], own[:half])
    on = (info[COUNTS + cols + at] > 0) & (at < cols - 1)
    own = jnp.where(on, factors[1, 0], identity)
    prev[...] = own[:, half:]
    cur[...] = own[:, :half]
    chain_b[...] = jnp.where(info[OWNS] == 1, own[:, :half], own[:, half:]).T


def pair_kernel(info, own, across, out):
    odd = info[ODD] == 1
    out[0] = jnp.where(odd, across[...], own[...])
    out[1] = jnp.where(odd, own[...], across[...])


def rest_kernel(info, *refs):
    del info, refs


def first_kernel(joint, info, seg, col, near, far, prev_top, *rest):
    sends, (last_top, col_h, col_l, carry) = rest[: 2 - joint], rest[2 - joint :]
    half = prev_top.shape[0]
    i = pl.program_id(0)

    @pl.when(i == 0)
    def _():
        col_h[...], col_l[...] = split(col[...])
        carry[...] = prev_top[...]

    mid = split(dot3(split(seg[...]), (col_h[...], col_l[...])))
    out = dot3(split(jnp.concatenate([near[...], far[...]], axis=0)), mid)
    sent = jnp.where(info[PLANE0] == 1, carry[...], out[:half])
    if joint:
        sends[0][0] = out[half:]
        sends[0][1] = sent
    else:
        sends[0][...] = out[half:]
        sends[1][...] = sent
    carry[...] = out[:half]
    last_top[...] = out[:half]


def second_kernel(begin, count, tail, older, turn, info, near, far, bottom, sent, got_bottom, got_top, *rest):
    left, right = rest[-2:]
    half = bottom.shape[0]

    @pl.when(pl.program_id(0) < count)
    def _():
        a, b = near[...], far[...]
        if older:
            late = info[LATE] == 1
            a, b = jnp.where(late, rest[-4][...], a), jnp.where(late, rest[-3][...], b)
        turned = info[turn] == 1
        lower, upper = split(jnp.where(turned, b, a)), split(jnp.where(turned, a, b))

        def stacked(one, other):
            return split(jnp.concatenate([one, other], axis=0))

        new_bottom = dot3(lower, stacked(bottom[...], got_top[...]))
        new_top = dot3(upper, stacked(got_bottom[...], sent[...]))
        passing = (info[PLANE0] == 1) & (begin + pl.program_id(0) == info[NEWEST] + 1)
        new_top = jnp.where(passing, sent[...], new_top)
        left[0] = new_bottom[:, :half]
        left[1] = new_top[:, :half]
        right[0] = new_bottom[:, half:]
        right[1] = new_top[:, half:]

    if tail:

        @pl.when(pl.program_id(0) == count)
        def _():
            left[0] = left[1] = rest[0][:, :half]
            right[0] = right[1] = rest[0][:, half:]


def split_columns(prev, cur, scratch):
    prev_h, prev_l, cur_h, cur_l = scratch
    prev_h[...], prev_l[...] = split(prev[...])
    cur_h[...], cur_l[...] = split(cur[...])


def columns(left_in, mine_left, mine_right, right_in, scratch, out):
    prev_h, prev_l, cur_h, cur_l = scratch
    half = mine_left.shape[1]

    def wide(one, other):
        return split(jnp.concatenate([one, other], axis=1))

    out[:, :half] = dot3(wide(left_in, mine_left), (prev_h[...], prev_l[...]))
    out[:, half:] = dot3(wide(mine_right, right_in), (cur_h[...], cur_l[...]))


def third_kernel(begin, last_unit, slots, none_far, again, info, left, right, up_far, up_near, down_near, down_far, down_last, prev, cur, held, out, *scratch):
    del held
    wanted = (info[LAST_IN] == 1) | (not again)
    *scratch, made, sems = scratch
    e, count = pl.program_id(0), made.shape[0]
    half = left.shape[1]

    def copies(unit):
        slot = lax.rem(info[NEWEST] - begin - unit + slots, slots)
        upper = lax.rem(slot + info[PLANE0], slots)
        for h, row in enumerate(((2 * slot + 1) * half, 2 * upper * half)):
            place = pl.ds(pl.multiple_of(row, half), half)
            yield pltpu.make_async_copy(made.at[unit, pl.ds(h * half, half)], out.at[place], sems.at[unit, h])

    @pl.when(e == 0)
    def _():
        split_columns(prev, cur, scratch)

    def flat(ref):
        return ref[...].reshape(2 * half, half)

    before = jnp.zeros((2 * half, half), jnp.float32) if none_far else flat(up_far)
    left_in = jnp.where(info[FIRST_IN] == 1, before, flat(up_near))
    far = flat(down_far)
    ends_here = (info[USE_LAST] == 1) & (begin + e == last_unit)
    far = jnp.concatenate([far[:half], jnp.where(ends_here, down_last[...], far[half:])], axis=0)
    right_in = jnp.where(info[LAST_IN] == 1, far, flat(down_near))
    for unit in range(count):

        @pl.when((e == unit) & wanted)
        def _():
            columns(left_in, flat(left), flat(right), right_in, scratch, made.at[unit])
            for copy in copies(unit):
                copy.start()

    @pl.when((e == count - 1) & wanted)
    def _():
        for unit in range(count):
            for copy in copies(unit):
                copy.wait()


def last_kernel(info, top, up_far, up_near, down_near, prev, cur, held, out, *scratch):
    del held
    half = top.shape[0]
    split_columns(prev, cur, scratch)
    left_in = jnp.where(info[FIRST_IN] == 1, up_far[...], up_near[...])
    columns(left_in, top[:, :half], top[:, half:], down_near[...], scratch, out)

def rows_kernel(above_blocks, info, above, basis, col, left, right, col_h, col_l):
    half = left.shape[1]
    i = pl.program_id(0)

    @pl.when(i == 0)
    def _():
        col_h[...], col_l[...] = split(col[...])

    rows = jnp.where(i < above_blocks, above[...], basis[...])
    out = dot3(split(rows), (col_h[...], col_l[...]))
    left[...] = out[:, :half]
    right[...] = out[:, half:]


def rows_end_kernel(info, left, right, left_in, right_in, prev, cur, out, *scratch):
    @pl.when(pl.program_id(0) == 0)
    def _():
        split_columns(prev, cur, scratch)

    columns(left_in[...], left[...], right[...], right_in[...], scratch, out)


def whole(shape):
    return pl.BlockSpec(shape, lambda *_: (0,) * len(shape))


def body(segment, above_rows, basis_rows, factors, swap_counts):
    slots = segment.shape[0]
    window = segment.shape[2]
    half = window // 2
    planes = lax.axis_size("prow")
    cols = lax.axis_size("pcol")
    plane = lax.axis_index("prow")
    col = lax.axis_index("pcol")
    f32, bf = jnp.float32, jnp.bfloat16
    paired = planes == 2
    fold = next(size for size in (4, 2, 1) if slots % size == 0) if paired else 1
    group = planes * fold
    levels = slots // fold
    level = col // group
    newest = fold * level + fold - 1
    owner = plane if paired else (plane + planes - 1) % planes
    member = col % planes
    place = [
        plane,
        col,
        plane == 0,
        newest,
        member,
        (member != plane) & paired,
        col % group == 0,
        col % group == group - 1,
        level == levels - 1,
        (plane == 0) & (level == levels - 2),
        member == plane,
        (col // 2) % 2,
        (col // 4) % 2 == 0,
    ]
    info = jnp.concatenate([jnp.stack([jnp.asarray(v, jnp.int32) for v in place]), swap_counts.reshape(-1)])

    def send(value, route):
        return lax.ppermute(value, GRID, [(a * cols + b, c * cols + d) for (a, b), (c, d) in route])

    everyone = [(p, c) for p in range(planes) for c in range(cols)]

    def along(value, step, wanted=lambda c: True):
        route = [((p, c), (p, c + step)) for p, c in everyone if 0 <= c + step < cols and wanted(c)]
        return send(value, route)

    def shape(*dims):
        return jax.ShapeDtypeStruct(dims, f32)

    last = []

    if paired:
        raw = factors[0, 0]
        came = send(raw, [((p, c), (p, c + 1 - 2 * p)) for p, c in everyone if c % 2 == p])
    else:
        came = factors[0, 0]
    own_first, full_first, half_a, chain_b, prev_own, cur = call(
        functools.partial(factor_kernel, paired, cols),
        info,
        (1,),
        [whole((2, 1, window, window)), whole((window, window))],
        [whole((window, window)), whole((2, half, window))]
        + [whole((half, window))] * 2
        + [whole((window, half))] * 2,
        [shape(window, window), shape(2, half, window)] + [shape(half, window)] * 2 + [shape(window, half)] * 2,
        [],
        (factors, came),
    )
    last.append(own_first)
    rows = lax.broadcasted_iota(jnp.int32, (window, half), 0)
    lanes = lax.broadcasted_iota(jnp.int32, (window, half), 1)

    def hopped(value, hop):
        return along(value, group, lambda c: c // group >= hop - 1)

    def chained(value):
        values = [value]
        for hop in range(1, levels):
            values.append(hopped(values[-1], hop))
        return values

    teams = [list(range(g * group, (g + 1) * group)) for g in range(cols // group)]

    def gathered(value):
        mine = lax.all_gather(value, "pcol", axis_index_groups=teams)
        return (mine, lambda q: 2 * q, mine, lambda q: 2 * q + 1)

    def placed_all(values, *after):
        anywhere = [pl.BlockSpec(memory_space=pl.ANY)] * len(values)
        shapes = [shape(*value.shape) for value in values]
        alias = {1 + k: k for k in range(len(values))}
        values = call(rest_kernel, info, (1,), anywhere, anywhere, shapes, [], values, alias, [*last[-1:], *after])
        last.append(values[0])
        return values

    def placed(value, *after):
        return placed_all([value], *after)[0]

    def paired_up(own, across, *after):
        out = call(
            pair_kernel,
            info,
            (1,),
            [whole((half, window))] * 2,
            whole((2, half, window)),
            shape(2, half, window),
            [],
            (own, across),
            after=[*last[-1:], *after],
        )
        last.append(out)
        return out

    def with_swapped(mine):
        other = send(mine, [((p, c), (p, c + 1 - 2 * (c % 2))) for p, c in everyone])
        return (mine, lambda q: q % 2, other, lambda q: q % 2)

    if not paired:

        def shared(value, holder):
            value = jnp.where(member == holder, value, jnp.zeros_like(value))
            return lax.psum(value, "pcol", axis_index_groups=teams)

        full_first = shared(full_first, plane)
        both = jnp.stack([shared(chain_b, plane), shared(chain_b, owner)])
        first_factors = [(value, lambda q: 0, value, lambda q: 1) for value in chained(full_first)]
        second_factors = [(value, lambda q: 0, value, lambda q: 1) for value in chained(both) for _ in range(fold)]

    def previous(value):
        came_prev = along(value, 1)
        return came_prev, jnp.where(col == 0, (rows == lanes + half).astype(f32), came_prev)

    seg = segment.reshape(slots * window, window)

    def slot_of(t, f):
        return lax.rem(f[NEWEST] - t + slots, slots)

    def factor_specs(factor, at):

        def spec(array, first):
            return pl.BlockSpec((None, half, window), lambda i, f: (first(at(i)), 0, 0))

        return [spec(*factor[:2]), spec(*factor[2:])]

    def first_step(batch, prev_top, joint, after):
        count, begin = len(batch), batch[0]
        factor = first_factors[begin // fold] if begin or not paired else (full_first, lambda q: 0, full_first, lambda q: 1)
        place = 0 if begin == 0 else fold - 1 - begin % fold
        if joint:
            specs = [pl.BlockSpec((None, 2, half, window), lambda i, f: (i, 0, 0, 0))]
            shapes = [shape(count, 2, half, window)]
        else:
            specs = [pl.BlockSpec((None, None, half, window), lambda i, f: (i, 0, 0, 0))] * 2
            shapes = [shape(count, 1, half, window)] * 2
        outs = call(
            functools.partial(first_kernel, joint),
            info,
            (count,),
            [
                pl.BlockSpec((window, window), lambda i, f: (slot_of(begin + i, f), 0)),
                whole((window, window)),
                *factor_specs(factor, lambda i: place - i),
                whole((half, window)),
            ],
            specs + [whole((half, window))],
            shapes + [shape(half, window)],
            [pltpu.VMEM((window, window), bf)] * 2 + [pltpu.VMEM((half, window), f32)],
            (seg, own_first, factor[0], factor[2], prev_top),
            after=[*last[-1:], *after],
        )
        return outs[:-1], outs[-1]

    def exchange(batch, sends):
        down, up = [], []
        for p, c in everyone:
            places = [fold * (c // group) + fold - 1 - t for t in batch]
            tiles = [at * planes + p for at in places if at >= 0]
            if any(tile <= c and tile < cols - 1 for tile in tiles):
                down.append(((p, c), ((p + 1) % planes, c)))
            if any((tile if p else tile + planes) <= c for tile in tiles):
                up.append(((p, c), ((p - 1) % planes, c)))
        if len(sends) == 1:
            return [send(sends[0], sorted(set(down + up)))]
        return [send(sends[0], down), send(sends[1], up)]

    def second_step(batch, size, at, sends, gots, held, ended, after):
        count, begin = len(batch), batch[0]
        factor, place = second_factors[begin], fold - 1 - begin % fold
        older = second_factors[begin - 2] if by_level and begin == 2 else ()
        turn = PLANE if paired and not (by_level and begin < fold) else SWAP_B
        specs = lambda factor: factor_specs(factor, lambda i: place - inner(i)) if factor else []
        inner = lambda i: jnp.minimum(i, count - 1)
        piece = lambda k: pl.BlockSpec((None, None, half, window), lambda i, f: (inner(i), k, 0, 0))
        pieces = [piece(0), piece(len(sends) % 2)]
        ends = [pl.BlockSpec((2, half, half), lambda i, f: (at + i, 0, 0))] * 2
        extra = [whole((half, window))] if ended else [pl.BlockSpec(memory_space=pl.ANY)] * len(held)
        return call(
            functools.partial(second_kernel, begin, count, bool(ended), bool(older), turn),
            info,
            (count + len(ended),),
            specs(factor) + pieces + pieces + extra + specs(older),
            ends,
            [shape(2 * size, half, half)] * 2,
            [],
            (factor[0], factor[2], sends[0], sends[-1], gots[0], gots[-1], *ended, *held, *older[::2]),
            {7 + k: k for k in range(len(held))},
            [*last[-1:], *after],
        )

    split_scratch = [pltpu.VMEM((window, half), bf)] * 4

    counts = (above_rows.shape[0], basis_rows.shape[0])
    deep = window if all(n % window == 0 for n in counts) else half
    above_blocks, basis_blocks = (n // deep for n in counts)

    def rows_step(after=()):
        tall = pl.BlockSpec((deep, half), lambda i, f: (i, 0))
        blocks = above_blocks + basis_blocks
        return call(
            functools.partial(rows_kernel, above_blocks),
            info,
            (blocks,),
            [
                pl.BlockSpec((deep, window), lambda i, f: (jnp.minimum(i, above_blocks - 1), 0)),
                pl.BlockSpec((deep, window), lambda i, f: (jnp.maximum(i - above_blocks, 0), 0)),
                whole((window, window)),
            ],
            [tall] * 2,
            [shape(blocks * deep, half)] * 2,
            [pltpu.VMEM((window, window), bf)] * 2,
            (above_rows, basis_rows, own_first),
            after=[*last[-1:], *after],
        )

    def rows_end(first, blocks, parts, after):
        tall = pl.BlockSpec((deep, half), lambda i, f: (first + i, 0))
        return call(
            rows_end_kernel,
            info,
            (blocks,),
            [tall] * 4 + [whole((window, half))] * 2,
            pl.BlockSpec((deep, window), lambda i, f: (i, 0)),
            shape(blocks * deep, window),
            split_scratch,
            (*parts, prev, cur),
            after=[*last[-1:], *after],
        )

    lefts, rights, ups, downs = ([None] * slots for _ in range(4))

    def third_step(batch, held, after, early, again):
        begin = batch[0]
        fresh = held is None
        parts = [lefts[begin], rights[begin]]
        parts.append(ups[begin - fold] if begin >= fold else ups[begin])
        parts += [ups[begin], downs[begin], downs[begin if early else (begin + fold) % slots]]
        step = lambda e, f: e * f[LAST_IN] if again else e
        piece = lambda at: pl.BlockSpec((2, half, half), lambda e, f: (at + step(e, f), 0, 0))
        args = [array for array, _ in parts]
        ending = slots - fold in batch
        tail_row = 2 * ending_strips[2] if ending else 0
        return call(
            functools.partial(third_kernel, begin, slots - fold, slots, begin < fold, again),
            info,
            (len(batch),),
            [piece(at) for _, at in parts]
            + [pl.BlockSpec((None, half, half), lambda e, f: (tail_row, 0, 0))]
            + [whole((window, half))] * 2
            + [pl.BlockSpec(memory_space=pl.ANY)],
            pl.BlockSpec(memory_space=pl.ANY),
            shape(*seg.shape),
            split_scratch
            + [pltpu.VMEM((len(batch), window, window), f32), pltpu.SemaphoreType.DMA((len(batch), 2))],
            (*args, ending_strips[1] if ending else args[0], prev, cur, args[0] if fresh else held),
            None if fresh else {10: 0},
            [*last[-1:], *after],
        )

    def last_step(held):
        quarter = lambda at: pl.BlockSpec((None, half, half), lambda i, f: (at, 0, 0))
        array, at = ups[slots - fold]

        def out_block(i, f):
            return (jnp.where((f[LAST_LEVEL] == 1) & (f[PLANE0] == 1), 0, 2 * slot_of(slots - 1, f) + 1), 0)

        return call(
            last_kernel,
            info,
            (1,),
            [whole((half, window)), quarter(2 * at + 1)] + [quarter(2 * ending_strips[2])] * 2
            + [whole((window, half))] * 2
            + [pl.BlockSpec(memory_space=pl.ANY)],
            pl.BlockSpec((half, window), out_block),
            shape(*seg.shape),
            split_scratch,
            (tops[-1], array, *ending_strips[:2], prev, cur, held),
            {7: 0},
            last[-1:],
        )

    tops, sent, got, made = [jnp.zeros((half, window), f32)], {}, {}, {}

    def do_first(batch, after=()):
        sent[batch[0]], top = first_step(batch, tops[-1], paired, after)
        tops.append(top)
        last.append(top)
        got[batch[0]] = exchange(batch, sent[batch[0]])

    def do_second(batch, strip, ended=(), after=()):
        begin = batch[0]
        held = made.get(strip[0], ())
        made[strip[0]] = second_step(
            batch, len(strip) + len(ended), begin - strip[0], sent[begin], got[begin], held, ended, after
        )
        last.append(made[strip[0]][0])
        if batch[-1] == strip[-1]:
            left, right = made[strip[0]]


            def filled(c):
                first = fold * (c // group) + fold - 1
                return any(-1 <= first - t <= c // planes for t in strip)

            up, down = along(right, 1, filled), along(left, -1, filled)
            for place, t in enumerate(strip):
                lefts[t], rights[t] = (left, place), (right, place)
                ups[t], downs[t] = (up, place), (down, place)
            return up, down, len(strip)

    out = [None]

    def do_third(batch, early=False, again=False):
        out[0] = third_step(batch, out[0], (), early, again)
        last.append(out[0])

    def do_last():
        out[0] = last_step(out[0])
        last.append(out[0])

    def do_rows(after=()):
        left, right = rows_step(after)
        last.append(left)
        return left, right, along(right, 1), along(left, -1)

    def do_rows_end(which, after=()):
        first, blocks = ((0, above_blocks), (above_blocks, basis_blocks))[which]
        row_ends.append(rows_end(first, blocks, parts, after))
        last.append(row_ends[-1])

    row_ends = []
    def hop(value, distance):
        return along(value, group // 2, lambda c: c // (group // 2) >= distance - 1)

    by_level = paired and fold == 4 and levels == 2
    if by_level:
        first_factors = [gathered(half_a)]
        hop_a = hopped(half_a, 1)
        across = send(chain_b, [((p, c), (p, c // 4 * 4 + (c + 2) % 4)) for p, c in everyone])
        do_first([0])
        came_prev, prev = previous(prev_own)
        pieces = paired_up(chain_b, across, came_prev)
        second_factors = [with_swapped(pieces)] * 2
        pieces = hop(pieces, 1)
        do_first([1], got[0])
        first_factors.append(gathered(placed(hop_a)))
        do_first([2, 3], [second_factors[0][2]])
        pieces, passed_b = placed_all([pieces, chain_b])
        second_factors += [with_swapped(pieces)] * 2
        hop_b = hopped(passed_b, 1)
        do_second([0], [0, 1, 2, 3], after=got[1])
        parts = do_rows([second_factors[2][2]])
        do_second([1], [0, 1, 2, 3])
        do_first([4, 5], got[2])
        second_factors += [gathered(placed(hop_b))] * fold
        do_second([2, 3], [0, 1, 2, 3], after=parts[2:3])
        do_first([6, 7], parts[3:])
        do_rows_end(0)
        do_rows_end(1)
        got[4] = [placed(got[4][0])]
        ending_strips = do_second([4, 5], [4, 5], ended=[tops[-1]])
        do_third([0, 1], early=True)
        do_second([6, 7], [6, 7])
        do_third([2, 3], early=True)
        do_third([4, 5])
        do_third([0, 1], again=True)
        do_last()
        do_third([6, 7])
        do_third([2, 3], again=True)
    else:
        _, prev = previous(prev_own)
        parts = do_rows()
        if paired:
            first_factors = [gathered(value) for value in chained(half_a)]
            second_factors = [gathered(value) for value in chained(chain_b) for _ in range(fold)]
        for t in range(slots):
            do_first([t])
        for t in range(slots):
            ending_strips = do_second([t], [t], ended=[tops[-1]] if t == slots - 1 else ())
        for t in range(slots - 1):
            do_third([t])
        do_last()
        do_third([slots - 1])
        do_rows_end(0)
        do_rows_end(1)
    return (out[0].reshape(segment.shape), *row_ends)


def solution(mesh):
    placed = (
        P(None, "prow", None, "pcol"),
        P("prow", "pcol"),
        P("prow", "pcol"),
        P(None, "pcol", None, None),
        P(),
    )
    return jax.shard_map(
        body,
        mesh=mesh,
        in_specs=placed,
        out_specs=(P(None, "prow", None, "pcol"), P("prow", "pcol"), P("prow", "pcol")),
        check_vma=False,
    )
```
